128 devices in a mesh: rep: 4 (over x_hi, core), shard: 32 (over y, x_lo, z).
Axes of the slice: x: 4 (x_hi: 2, x_lo: 2; x = x_hi * 2 + x_lo), y: 4, z: 4, core: 2. Of those that a mesh axis runs over, the one named last changes fastest.
Arguments:
- hidden: bfloat16 [32768, 8192], P(('rep', 'shard')), may hold values from -6 to 6
- seg_ids: int32 [128, 256], P(('rep', 'shard')), may hold values from 0 to 15, never falling along the last dimension, each value on 1 to 32 neighbouring positions
- ranks: int32 [128, 2, 8], P(('rep', 'shard')), may hold values from 0 to 7, each once within a row
- adapter_in: bfloat16 [3, 8192, 128], P(None, 'shard'), may hold values from -0.0625 to 0.0625
- adapter_out: bfloat16 [3, 128, 8192], P(None, None, 'shard'), may hold values from -0.5 to 0.5
- score_head: bfloat16 [8192], P('shard'), may hold values from -0.25 to 0.25
- final_gain: bfloat16 [8192], P('shard'), may hold values from 0.5 to 1.5
Outputs:
- grad_in: float32 [3, 8192, 128], P(None, 'shard')
- grad_out: float32 [3, 128, 8192], P(None, None, 'shard')
- grad_head: float32 [8192], P('shard')
- grad_gain: float32 [8192], P('shard')
The draws below stay inside these ranges and needn't reach their ends.
Inputs may be any that keep to these rules, and one draw needn't show every extreme that they name: Each row of ranks orders the 8 responses of one list, best first.
All inputs are finite; a program needn't handle non-finite values.
Results may differ from the reference program's by a relative error of at most 0.034.
Values may be sent and summed in bfloat16 or wider, within the bound.
A program may use at most 128 MiB of HBM per device.

```python
import math
import jax
import jax.numpy as jnp
import numpy as np
from jax import lax

D = 8192
R = 128
LAYERS = 3
K = 8
SEG_MOST = 32
TOK_DEV = 256
LISTS = 2
SEGS = 16
BLOCKS = 128
TOKENS = 32768


def block_levels(stream_key, dims, pieces, smallest, largest):
    loudness, own = 1.0, jax.random.fold_in(stream_key, 6)
    for axis_at, blocks in pieces:
        steps = jnp.exp(jax.random.uniform(jax.random.fold_in(own, axis_at), (blocks,), jnp.float32, smallest / len(pieces), largest / len(pieces)))
        loudness = loudness * jnp.repeat(steps, dims[axis_at] // blocks).reshape([-1 if axis == axis_at else 1 for axis in range(len(dims))])
    return loudness


def length_profile(number_of, total, bound, lean):
    portions = [(1 << 20) // math.isqrt(rank ** lean) + 1 for rank in range(2, number_of + 1)]
    spare, given = total - bound - (number_of - 1), [1] * (number_of - 1)
    while spare > 0:
        candidates = [i for i in range(number_of - 1) if given[i] < bound]
        pool, left = sum([portions[i] for i in candidates]), spare
        for i in candidates:
            extra = min(bound - given[i], max(1, left * portions[i] // pool), spare)
            given[i] = given[i] + extra
            spare = spare - extra
    return np.array([bound] + given)


def uneven_parts(key, amount, total, limit, skew):
    if amount == 2:
        one = jax.random.randint(key, (), max(1, total - limit), min(limit, total - 1) + 1)
        return jnp.stack([one, total - one])
    sizes = jnp.asarray(length_profile(amount, total, limit, skew), jnp.int32)
    couples = (amount - 1) // 2
    giver, taker = sizes[1:1 + 2 * couples:2], sizes[2:2 + 2 * couples:2]
    margin = jnp.minimum(giver - 1, limit - taker)
    shifted = jax.random.randint(jax.random.fold_in(key, 1), (couples,), 0, 1 << 20) % (margin + 1)
    sizes = sizes.at[1:1 + 2 * couples:2].set(giver - shifted).at[2:2 + 2 * couples:2].set(taker + shifted)
    return sizes[jax.random.permutation(jax.random.fold_in(key, 2), amount)]


def centred(key, extent, scale, most, split=(), kind=jnp.bfloat16):
    values = scale * jax.random.normal(key, extent, jnp.float32)
    if split:
        values = values * block_levels(key, extent, split, -0.22, 0.18)
    return jnp.clip(values, -most, most).astype(kind)


def setup_inputs(seed: int = 0) -> dict:
    key_of = jax.random.split(jax.random.key(seed), 8)
    hidden = centred(key_of[0], (TOKENS, D), 1.0, 6.0, ((0, 128),))
    seg_ids = jax.vmap(lambda own: jnp.searchsorted(jnp.cumsum(uneven_parts(own, SEGS, TOK_DEV, SEG_MOST, 1)), jnp.arange(TOK_DEV), side="right"))(jax.random.split(key_of[1], BLOCKS)).reshape((BLOCKS, TOK_DEV)).astype(jnp.int32)
    ranks = jax.vmap(lambda own: jax.random.permutation(own, K))(jax.random.split(key_of[2], BLOCKS * LISTS)).reshape((BLOCKS, LISTS, K)).astype(jnp.int32)
    adapter_in = centred(key_of[3], (LAYERS, D, R), D ** -0.5, 0.0625, ((1, 32),))
    adapter_out = centred(key_of[4], (LAYERS, R, D), R ** -0.5, 0.5, ((2, 32),))
    score_head = centred(key_of[5], (D,), (D // 16) ** -0.5, 0.25, ((0, 32),))
    final_gain = jnp.clip(1.0 + 0.1 * jax.random.normal(key_of[6], (D,), jnp.float32), 0.5, 1.5).astype(jnp.bfloat16)
    return {"hidden": hidden, "seg_ids": seg_ids, "ranks": ranks, "adapter_in": adapter_in, "adapter_out": adapter_out, "score_head": score_head, "final_gain": final_gain}


EPS = 1e-06

def norm_rows(values):
    rinv = lax.rsqrt(lax.optimization_barrier(jnp.mean(values * values, axis=-1, keepdims=True)) + EPS)
    return (values * rinv, rinv)

def layer_forward(state, w_in, w_out):
    values = state.astype(jnp.float32)
    normed, rinv = norm_rows(values)
    unit = normed.astype(jnp.bfloat16)
    inner = jnp.dot(unit, w_in, preferred_element_type=jnp.float32)
    active = jax.nn.silu(inner).astype(jnp.bfloat16)
    outer = jnp.dot(active, w_out, preferred_element_type=jnp.float32)
    return ((values + outer).astype(jnp.bfloat16), (state, unit, inner, active))

def layer_backward(upper, saved, w_in, w_out):
    state, unit, inner, active = saved
    normed, rinv = norm_rows(state.astype(jnp.float32))
    grad_b = lax.dot_general(active, upper, (((0,), (0,)), ((), ())), preferred_element_type=jnp.float32)
    d_active = lax.dot_general(upper, w_out, (((1,), (1,)), ((), ())), preferred_element_type=jnp.float32)
    sigm = jax.nn.sigmoid(inner)
    d_inner = (d_active * sigm * (1.0 + inner * (1.0 - sigm))).astype(jnp.bfloat16)
    grad_a = lax.dot_general(d_inner, unit, (((0,), (0,)), ((), ())), preferred_element_type=jnp.float32)
    d_unit = lax.dot_general(d_inner, w_in, (((1,), (1,)), ((), ())), preferred_element_type=jnp.float32)
    d_state = rinv * (d_unit - normed * lax.optimization_barrier(jnp.mean(d_unit * normed, axis=-1, keepdims=True)))
    lower = (upper.astype(jnp.float32) + d_state).astype(jnp.bfloat16)
    return (lower, grad_a, grad_b)

def head_backward(state, segment, order, head, gain, n_lists, n_resp):
    values = state.astype(jnp.float32)
    normed, rinv = norm_rows(values)
    gain_f = gain.astype(jnp.float32)
    head_f = head.astype(jnp.float32)
    feats = normed * gain_f[None, :]
    n_segs = n_lists * n_resp
    onehot = (segment[None, :] == jnp.arange(n_segs, dtype=jnp.int32)[:, None]).astype(jnp.float32)
    counts = lax.optimization_barrier(jnp.sum(onehot, axis=1))
    pooled = jnp.dot(onehot, feats, precision=lax.Precision.HIGHEST) / counts[:, None]
    reward = jnp.dot(pooled, head_f, precision=lax.Precision.HIGHEST).reshape(n_lists, n_resp)
    select = (order[:, :, None] == jnp.arange(n_resp, dtype=jnp.int32)[None, None, :]).astype(jnp.float32)
    placed = lax.optimization_barrier(jnp.sum(select * reward[:, None, :], axis=-1))
    expo = jnp.exp(placed)
    suffix = jnp.flip(jnp.cumsum(jnp.flip(expo, -1), axis=-1), -1)
    prefix = jnp.cumsum(1.0 / suffix, axis=-1)
    d_placed = -1.0 + expo * prefix
    d_reward = lax.optimization_barrier(jnp.sum(select * d_placed[:, :, None], axis=1)).reshape(n_segs)
    grad_head = jnp.dot(d_reward, pooled, precision=lax.Precision.HIGHEST)
    coeff = jnp.dot(d_reward / counts, onehot, precision=lax.Precision.HIGHEST)
    d_feats = coeff[:, None] * head_f[None, :]
    grad_gain = lax.optimization_barrier(jnp.sum(d_feats * normed, axis=0))
    d_normed = d_feats * gain_f[None, :]
    d_state = rinv * (d_normed - normed * lax.optimization_barrier(jnp.mean(d_normed * normed, axis=-1, keepdims=True)))
    return (d_state.astype(jnp.bfloat16), grad_head, grad_gain)

def reference(hidden, seg_ids, ranks, adapter_in, adapter_out, score_head, final_gain):
    n_blocks = seg_ids.shape[0]
    tok_block = seg_ids.shape[1]
    n_lists = ranks.shape[1]
    n_resp = ranks.shape[2]
    n_layers = adapter_in.shape[0]
    blocks = hidden.reshape(n_blocks, tok_block, hidden.shape[1])

    def one_block(carry, items):
        state, segment, order = items
        saved_all = []
        for layer in range(n_layers):
            state, saved = layer_forward(state, adapter_in[layer], adapter_out[layer])
            saved_all.append(saved)
        upper, g_head, g_gain = head_backward(state, segment, order, score_head, final_gain, n_lists, n_resp)
        acc_a, acc_b, acc_h, acc_g = carry
        parts_a = []
        parts_b = []
        for layer in range(n_layers - 1, -1, -1):
            upper, grad_a, grad_b = layer_backward(upper, saved_all[layer], adapter_in[layer], adapter_out[layer])
            parts_a.append(grad_a)
            parts_b.append(grad_b)
        stack_a = jnp.stack(parts_a[::-1])
        stack_b = jnp.stack(parts_b[::-1])
        return ((acc_a + stack_a, acc_b + stack_b, acc_h + g_head, acc_g + g_gain), None)
    width = hidden.shape[1]
    rank_b = adapter_in.shape[2]
    start = (jnp.zeros((n_layers, rank_b, width), jnp.float32), jnp.zeros((n_layers, rank_b, width), jnp.float32), jnp.zeros((width,), jnp.float32), jnp.zeros((width,), jnp.float32))
    final, unused = lax.scan(one_block, start, (blocks, seg_ids, ranks))
    acc_a, acc_b, acc_h, acc_g = final
    return (jnp.transpose(acc_a, (0, 2, 1)), acc_b, acc_h, acc_g)
```

```python
import jax
import jax.numpy as jnp
from jax import lax
from jax.experimental import pallas as pl
from jax.experimental.pallas import tpu as pltpu
from jax.sharding import PartitionSpec as P

EPS = 1e-06
MESH = pl.DeviceIdType.MESH
F32 = jnp.float32
BF16 = jnp.bfloat16
LAYERS = 3
WIDTH = 8192
TOK = 256
ROWS = 2 * TOK
R = 128
HALF = 128
EXTRA = 16
N_SEMS = 192
NT = (((1,), (1,)), ((), ()))
CHUNK = 256


def unit_rows(layer):
    return R + EXTRA if layer == LAYERS - 1 else R


def scratch():
    shapes = {}
    for level in range(LAYERS + 1):
        shapes["h", level] = pltpu.VMEM((4, 4, ROWS, 2 * HALF), BF16)
        shapes["sq", level] = pltpu.VMEM((ROWS, 128), F32)
        shapes["sq_in", level] = pltpu.VMEM((ROWS, 128), F32)
        shapes["rinv", level] = pltpu.VMEM((ROWS, 128), F32)
    for layer in range(LAYERS):
        rows = unit_rows(layer)
        shapes["own", layer] = pltpu.VMEM((rows, HALF), BF16)
        shapes["wa", layer] = pltpu.VMEM((4, 4, 2, HALF, R), BF16)
        shapes["wb", layer] = pltpu.VMEM((2, 4, 4, rows, HALF), BF16)
        shapes["z", layer] = pltpu.VMEM((ROWS, R), F32)
        shapes["z_in", layer] = pltpu.VMEM((ROWS, R), F32)
        shapes["act_t", layer] = pltpu.VMEM((R, ROWS), BF16)
        shapes["da", layer] = pltpu.VMEM((ROWS, R), F32)
        shapes["da_in", layer] = pltpu.VMEM((ROWS, R), F32)
        shapes["ga", layer] = pltpu.VMEM((2, 4, 4, R, HALF), BF16)
        shapes["ga1", layer] = pltpu.VMEM((2, 4, R, HALF), BF16)
        shapes["ga2", layer] = pltpu.VMEM((2, 2, 4, R, HALF), BF16)
        shapes["ga3", layer] = pltpu.VMEM((2, R, HALF), BF16)
        shapes["ga4", layer] = pltpu.VMEM((2, 2, R, HALF), BF16)
        shapes["ga5", layer] = pltpu.VMEM((R, HALF), BF16)
        shapes["ga6", layer] = pltpu.VMEM((2, 2, R, HALF), F32)
        shapes["gb", layer] = pltpu.VMEM((2, 4, 4, rows, HALF), BF16)
        shapes["gb1", layer] = pltpu.VMEM((4, 4, rows, HALF), BF16)
        shapes["gb2", layer] = pltpu.VMEM((4, rows, HALF), BF16)
        shapes["gb3", layer] = pltpu.VMEM((2, 4, rows, HALF), BF16)
        shapes["gb4", layer] = pltpu.VMEM((rows, HALF), BF16)
        shapes["gb5", layer] = pltpu.VMEM((2, rows, HALF), BF16)
        shapes["gb6", layer] = pltpu.VMEM((2, 2, rows, HALF), F32)
    shapes["act"] = pltpu.VMEM((ROWS, R), BF16)
    shapes["dzr"] = pltpu.VMEM((ROWS, R), BF16)
    shapes["dzr_t"] = pltpu.VMEM((R, ROWS), BF16)
    shapes["tok"] = pltpu.VMEM((ROWS, 128), F32)
    shapes["q"] = pltpu.VMEM((ROWS, 128), F32)
    shapes["q_in"] = pltpu.VMEM((ROWS, 128), F32)
    shapes["coef"] = pltpu.VMEM((ROWS, 128), F32)
    shapes["vec"] = pltpu.VMEM((16, ROWS), BF16)
    shapes["hg"] = pltpu.VMEM((4, 4, 8, 2 * HALF), F32)
    shapes["packs"] = pltpu.VMEM((2, 8, 256), F32)
    shapes["send"] = pltpu.SemaphoreType.DMA((N_SEMS,))
    shapes["recv"] = pltpu.SemaphoreType.DMA((N_SEMS,))
    shapes["local"] = pltpu.SemaphoreType.DMA((16,))
    return shapes


def kernel(hidden, w_in, w_out, pack, grad_in, grad_out, grad_vec, *refs):
    s = dict(zip(scratch(), refs))
    rep, shard = lax.axis_index("rep"), lax.axis_index("shard")
    xh, c = rep // 2, rep % 2
    y, xl, z = shard // 8, (shard // 4) % 2, shard % 4
    other = 1 - c
    p, q = y * other + z * c, z * other + y * c
    pp, p2, pm = (p + 1) % 4, (p + 2) % 4, (p + 3) % 4
    qp, q2, qm = (q + 1) % 4, (q + 2) % 4, (q + 3) % 4

    def at(y_by, z_by):
        return (rep, (y + y_by) % 4 * 8 + xl * 4 + (z + z_by) % 4)

    def along_x(by):
        x = (xh * 2 + xl + by) % 4
        return (x // 2 * 2 + c, y * 8 + x % 2 * 4 + z)

    to_pp, to_pm = at(other, c), at(3 * other, 3 * c)
    to_qp, to_qm = at(c, other), at(3 * c, 3 * other)
    to_xp, to_xm = along_x(1), along_x(3)
    to_pair = (rep, y * 8 + (1 - xl) * 4 + z)
    to_core = (xh * 2 + other, shard)
    to_rep = ((1 - xh) * 2 + c, shard)
    to_both = ((1 - xh) * 2 + other, shard)

    used = [0, 0]
    started = []

    def send(src, dst, to):
        i = used[0]
        used[0] += 1
        copy = pltpu.make_async_remote_copy(
            src_ref=src,
            dst_ref=dst,
            send_sem=s["send"].at[i],
            recv_sem=s["recv"].at[i],
            device_id=to,
            device_id_type=MESH,
        )
        copy.start()
        started.append(copy)
        return copy

    def local(src, dst):
        copy = pltpu.make_async_copy(src, dst, s["local"].at[used[1]])
        used[1] += 1
        copy.start()
        return copy

    def arrived(*copies):
        for copy in copies:
            copy.wait_recv()

    mine = pl.ds(pl.multiple_of(c * HALF, HALF), HALF)
    my_rows = pl.ds(pl.multiple_of(c * TOK, TOK), TOK)
    their_rows = pl.ds(pl.multiple_of(other * TOK, TOK), TOK)
    local_in = [
        local(w_in.at[l, mine], s["wa", l].at[p, q, xl]) for l in range(LAYERS)
    ]
    local_out = [
        local(w_out.at[l, :, mine], s["own", l].at[pl.ds(0, R)]) for l in range(LAYERS)
    ]

    barrier = pltpu.get_barrier_semaphore()
    partners = (to_pp, to_pm, to_qp, to_qm, to_xp, to_xm, to_core, to_rep, to_both)
    for partner in partners:
        pl.semaphore_signal(barrier, inc=1, device_id=partner, device_id_type=MESH)

    hidden_sem = s["local"].at[15]

    def load_hidden(i, carry):
        yy, zz = i // 4, i % 4
        for xx in range(2):
            col = pl.multiple_of(yy * 2048 + xx * 1024 + zz * 256 + c * HALF, HALF)
            pltpu.make_async_copy(
                hidden.at[:, pl.ds(col, HALF)],
                s["h", 0].at[yy * other + zz * c, zz * other + yy * c, my_rows, pl.ds(xx * HALF, HALF)],
                hidden_sem,
            ).start()
        return carry

    lax.fori_loop(0, 16, load_hidden, 0)
    pl.semaphore_wait(barrier, len(partners))

    def gather_in(l):
        w = s["wa", l]
        a = send(w_in.at[l, mine], w.at[p, q, xl], to_pair)
        yield
        local_in[l].wait()
        arrived(a)
        a = send(w.at[p, q], w.at[p, q], to_qp)
        b = send(w.at[p, q], w.at[p, q], to_qm)
        yield
        arrived(a, b)
        a = send(w.at[p, qm, 0], w.at[p, qm, 0], to_qp)
        b = send(w.at[p, qp, 1], w.at[p, qp, 1], to_qm)
        yield
        arrived(a, b)
        a = send(w.at[p], w.at[p], to_pp)
        b = send(w.at[p], w.at[p], to_pm)
        yield
        arrived(a, b)
        a = send(w.at[pm, pl.ds(0, 2)], w.at[pm, pl.ds(0, 2)], to_pp)
        b = send(w.at[pp, pl.ds(2, 2)], w.at[pp, pl.ds(2, 2)], to_pm)
        yield
        arrived(a, b)
        yield

    def gather_out(l):
        w, own, rows = s["wb", l], s["own", l], unit_rows(l)
        low, high = pl.ds(0, 64), pl.ds(64, rows - 64)
        local_out[l].wait()
        if rows > R:
            head, gain = pack[0:1, :], pack[1:2, :]
            both = head * gain
            both = both[:, :HALF] * (1 - c).astype(F32) + both[:, HALF:] * c.astype(F32)
            hi = both.astype(BF16)
            lo = (both - hi.astype(F32)).astype(BF16)
            row = lax.broadcasted_iota(jnp.int32, (EXTRA, HALF), 0)
            own[pl.ds(R, EXTRA), :] = jnp.where(
                row == 0, hi.astype(F32), jnp.where(row == 1, lo.astype(F32), 0.0)
            ).astype(BF16)
        a = send(own, w.at[xl, p, q], to_pp)
        b = send(own, w.at[xl, p, q], to_pm)
        kept = local(own, w.at[xl, p, q])
        yield
        arrived(a, b)
        a = send(w.at[xl, pm, q, low], w.at[xl, pm, q, low], to_pp)
        b = send(w.at[xl, pp, q, high], w.at[xl, pp, q, high], to_pm)
        yield
        kept.wait()
        arrived(a, b)
        a = send(w.at[xl, :, q], w.at[xl, :, q], to_qp)
        b = send(w.at[xl, :, q], w.at[xl, :, q], to_qm)
        yield
        arrived(a, b)
        a = send(w.at[xl, pl.ds(0, 2), qm], w.at[xl, pl.ds(0, 2), qm], to_qp)
        b = send(w.at[xl, pl.ds(2, 2), qp], w.at[xl, pl.ds(2, 2), qp], to_qm)
        yield
        arrived(a, b)
        a = send(w.at[xl, pl.ds(0, 2)], w.at[xl, pl.ds(0, 2)], to_xp)
        b = send(w.at[xl, pl.ds(2, 2)], w.at[xl, pl.ds(2, 2)], to_xm)
        yield
        arrived(a, b)
        yield

    def add(ref, index, *others):
        total = ref[index].astype(F32)
        for more in others:
            total = total + more.astype(F32)
        ref[index] = total.astype(BF16)

    def finish(own, l, store):
        copies = [send(own.at[c, xh], own.at[c, xh], to) for to in (to_rep, to_core, to_both)]
        yield
        arrived(*copies)
        for half in range(2):
            store(l, half, own[half, 0] + own[half, 1])
        yield

    def scatter_out(l):
        g, rows = s["gb", l], unit_rows(l)
        r1, r2, r3, r4, r5, r6 = (s["gb%d" % i, l] for i in range(1, 7))
        low, high = pl.ds(0, 64), pl.ds(64, rows - 64)
        a = send(g.at[1 - xl, pl.ds(0, 2)], r1.at[pl.ds(0, 2)], to_xp)
        b = send(g.at[1 - xl, pl.ds(2, 2)], r1.at[pl.ds(2, 2)], to_xm)
        yield
        arrived(a, b)

        def add_x(i, carry):
            for j in range(4):
                add(g, (xl, i, j), r1[i, j])
            return carry

        lax.fori_loop(0, 4, add_x, 0)
        a = send(g.at[xl, pl.ds(0, 2), q2], r2.at[pl.ds(0, 2)], to_qp)
        b = send(g.at[xl, pl.ds(2, 2), q2], r2.at[pl.ds(2, 2)], to_qm)
        yield
        arrived(a, b)
        for i in range(2):
            add(g, (xl, i, qp), r2[i])
            add(g, (xl, i + 2, qm), r2[i + 2])
        a = send(g.at[xl, :, qp], r3.at[0], to_qp)
        b = send(g.at[xl, :, qm], r3.at[1], to_qm)
        yield
        arrived(a, b)
        for i in range(4):
            add(g, (xl, i, q), r3[0, i], r3[1, i])
        a = send(g.at[xl, p2, q, low], r4.at[low], to_pp)
        b = send(g.at[xl, p2, q, high], r4.at[high], to_pm)
        yield
        arrived(a, b)
        add(g, (xl, pp, q, low), r4[low])
        add(g, (xl, pm, q, high), r4[high])
        a = send(g.at[xl, pp, q], r5.at[0], to_pp)
        b = send(g.at[xl, pm, q], r5.at[1], to_pm)
        yield
        arrived(a, b)
        r6[c, xh] = g[xl, p, q].astype(F32) + r5[0].astype(F32) + r5[1].astype(F32)
        yield from finish(r6, l, store_out)

    def scatter_in(l):
        g = s["ga", l]
        r1, r2, r3, r4, r5, r6 = (s["ga%d" % i, l] for i in range(1, 7))
        low, high = pl.ds(0, 64), pl.ds(64, 64)
        a = send(g.at[:, p2, pl.ds(0, 2)], r1.at[:, pl.ds(0, 2)], to_pp)
        b = send(g.at[:, p2, pl.ds(2, 2)], r1.at[:, pl.ds(2, 2)], to_pm)
        yield
        arrived(a, b)
        for x in range(2):
            for j in range(2):
                add(g, (x, pp, j), r1[x, j])
                add(g, (x, pm, j + 2), r1[x, j + 2])
        a = send(g.at[:, pp], r2.at[0], to_pp)
        b = send(g.at[:, pm], r2.at[1], to_pm)
        yield
        arrived(a, b)
        for x in range(2):
            for j in range(4):
                add(g, (x, p, j), r2[0, x, j], r2[1, x, j])
        a = send(g.at[:, p, q2, low], r3.at[:, low], to_qp)
        b = send(g.at[:, p, q2, high], r3.at[:, high], to_qm)
        yield
        arrived(a, b)
        for x in range(2):
            add(g, (x, p, qp, low), r3[x, low])
            add(g, (x, p, qm, high), r3[x, high])
        a = send(g.at[:, p, qp], r4.at[0], to_qp)
        b = send(g.at[:, p, qm], r4.at[1], to_qm)
        yield
        arrived(a, b)
        for x in range(2):
            add(g, (x, p, q), r4[0, x], r4[1, x])
        a = send(g.at[1 - xl, p, q], r5, to_pair)
        yield
        arrived(a)
        r6[c, xh] = g[xl, p, q].astype(F32) + r5[...].astype(F32)
        yield from finish(r6, l, store_in)

    def store_in(l, half, total):
        grad_in[l, pl.ds(half * HALF, HALF), :] = total.T

    def store_out(l, half, total):
        lanes = pl.ds(half * HALF, HALF)
        grad_out[l, :, lanes] = total[:R]
        if unit_rows(l) > R:
            vec = total[R : R + 8]
            row = lax.broadcasted_iota(jnp.int32, (8, HALF), 0)
            vec = jnp.sum(jnp.where(row == 0, vec, 0.0), axis=0, keepdims=True)
            grad_vec[0:1, lanes] = vec * pack[1:2, lanes]
            grad_vec[1:2, lanes] = vec * pack[0:1, lanes]

    def go(*jobs):
        for job in jobs:
            next(job, None)

    def lanes2(values):
        return jnp.concatenate([values, values], axis=1)

    def weights_out(l, i, j):
        w = s["wb", l]
        return jnp.concatenate([w[0, i, j, pl.ds(0, R)], w[1, i, j, pl.ds(0, R)]], axis=1)

    def squares(level):
        h, out = s["h", level], s["sq", level]
        out[...] = jnp.zeros_like(out)

        def step(i, carry):
            for r in range(0, ROWS, CHUNK):
                rows = pl.ds(r, CHUNK)
                total = out[rows, :]
                for j in range(4):
                    v = h[i, j, rows, :].astype(F32)
                    v = v * v
                    total = total + (v[:, :128] + v[:, 128:])
                out[rows, :] = total
            return carry

        lax.fori_loop(0, 4, step, 0)

    def down(l):
        h, w, out = s["h", l], s["wa", l], s["z", l]
        out[...] = jnp.zeros_like(out)

        def step(i, carry):
            lhs = jnp.concatenate([h[i, j] for j in range(4)], axis=1)
            out[...] += jnp.dot(lhs, w[i].reshape(4 * 2 * HALF, R), preferred_element_type=F32)
            return carry

        lax.fori_loop(0, 4, step, 0)

    def inverse(level):
        total = jnp.sum(s["sq", level][...] + s["sq_in", level][...], axis=1, keepdims=True)
        inv = lax.rsqrt(total * (1.0 / WIDTH) + EPS)
        s["rinv", level][...] = jnp.broadcast_to(inv, (ROWS, 128))

    def activate(l):
        v = (s["z", l][...] + s["z_in", l][...]) * s["rinv", l][...]
        s["z_in", l][...] = v
        active = v * jax.nn.sigmoid(v)
        s["act"][...] = active.astype(BF16)
        s["act_t", l][...] = active.T.astype(BF16)

    def up(l):
        h, out, sq = s["h", l], s["h", l + 1], s["sq", l + 1]
        last = l == LAYERS - 1
        sq[...] = jnp.zeros_like(sq)
        if last:
            s["q"][...] = jnp.zeros_like(s["q"])

        def step(i, carry):
            for j in range(4):
                w = weights_out(l, i, j)
                if last:
                    hg = s["hg"][i, j, 0:1, :]
                for r in range(0, ROWS, CHUNK):
                    rows = pl.ds(r, CHUNK)
                    v = jnp.dot(s["act"][rows, :], w, preferred_element_type=F32)
                    v = (h[i, j, rows, :].astype(F32) + v).astype(BF16)
                    out[i, j, rows, :] = v
                    v = v.astype(F32)
                    if last:
                        t = v * hg
                        s["q"][rows, :] += t[:, :128] + t[:, 128:]
                    v = v * v
                    sq[rows, :] += v[:, :128] + v[:, 128:]
            return carry

        lax.fori_loop(0, 4, step, 0)

    def gains():
        w = s["wb", LAYERS - 1]

        def step(i, carry):
            for j in range(4):
                for x in range(2):
                    rows = w[x, i, j, pl.ds(R, EXTRA)].astype(F32)
                    both = jnp.sum(rows, axis=0, keepdims=True)
                    s["hg"][i, j, :, pl.ds(x * HALF, HALF)] = jnp.broadcast_to(both, (8, HALF))
            return carry

        lax.fori_loop(0, 4, step, 0)

    def head():
        inv = s["rinv", LAYERS][...]
        dot_q = jnp.sum(s["q"][...] + s["q_in"][...], axis=1, keepdims=True)
        n_q = dot_q * inv
        seg_row = lax.broadcasted_iota(jnp.int32, (16, TOK), 0).astype(F32)
        onehots, rewards, counts = [], [], []
        for core in range(2):
            onehot = (s["packs"][core, 2:3, :] == seg_row).astype(F32)
            count = jnp.sum(onehot, axis=1, keepdims=True)
            total = jnp.dot(
                onehot,
                n_q[core * TOK : (core + 1) * TOK],
                precision=lax.Precision.HIGHEST,
                preferred_element_type=F32,
            )
            onehots.append(onehot)
            counts.append(count)
            rewards.append(total / count)
        place = lax.broadcasted_iota(jnp.int32, (8, 128), 0)
        lane = lax.broadcasted_iota(jnp.int32, (8, 128), 1)
        real = lane < 8
        for core in range(2):
            d_reward = []
            for k in range(2):
                order = s["packs"][core, 3 + k : 4 + k, 0:128]
                chosen = jnp.where(real & (order == place.astype(F32)), 1.0, 0.0)
                reward = rewards[core][8 * k : 8 * k + 8]
                placed = jnp.sum(chosen * reward, axis=0, keepdims=True)
                expo = jnp.exp(placed)
                suffix = jnp.sum(
                    jnp.where(real & (lane >= place), expo, 0.0), axis=1, keepdims=True
                )
                prefix = jnp.sum(
                    jnp.where(place <= lane, 1.0 / suffix, 0.0), axis=0, keepdims=True
                )
                d_placed = -1.0 + expo * prefix
                d_reward.append(
                    jnp.sum(jnp.where(chosen > 0.0, d_placed, 0.0), axis=1, keepdims=True)
                )
            scaled = jnp.concatenate(d_reward, axis=0) / counts[core]
            coef = lax.dot_general(
                onehots[core],
                jnp.broadcast_to(scaled, (16, 128)),
                (((0,), (0,)), ((), ())),
                precision=lax.Precision.HIGHEST,
                preferred_element_type=F32,
            )
            rows = pl.ds(core * TOK, TOK)
            inv_c = inv[core * TOK : (core + 1) * TOK]
            first = coef * inv_c
            s["coef"][rows, :] = first
            s["tok"][rows, :] = (
                first * inv_c * inv_c * dot_q[core * TOK : (core + 1) * TOK] * (1.0 / WIDTH)
            )
        vec = s["coef"][...].T[:8]
        hi = vec.astype(BF16)
        lo = (vec - hi.astype(F32)).astype(BF16)
        s["vec"][...] = jnp.concatenate([hi.astype(F32), lo.astype(F32)], axis=0).astype(BF16)

    def top():
        h, g = s["h", LAYERS], s["gb", LAYERS - 1]

        def step(i, carry):
            row = lax.broadcasted_iota(jnp.int32, (EXTRA, 256), 0)
            for j in range(4):
                vec = jnp.dot(s["vec"][...], h[i, j], preferred_element_type=F32)
                vec = jnp.where(row == 0, vec[:8][0:1] + vec[8:][0:1], 0.0).astype(BF16)
                g[0, i, j, pl.ds(R, EXTRA)] = vec[:, :HALF]
                g[1, i, j, pl.ds(R, EXTRA)] = vec[:, HALF:]
                hg = s["hg"][i, j, 0:1, :]
                for r in range(0, ROWS, CHUNK):
                    rows = pl.ds(r, CHUNK)
                    v = h[i, j, rows, :].astype(F32)
                    v = lanes2(s["coef"][rows, :]) * hg - v * lanes2(s["tok"][rows, :])
                    h[i, j, rows, :] = v.astype(BF16)
            return carry

        lax.fori_loop(0, 4, step, 0)

    def back_up(l):
        g, out = s["h", LAYERS], s["da", l]
        out[...] = jnp.zeros_like(out)

        def step(i, carry):
            lhs = jnp.concatenate([g[i, j] for j in range(4)], axis=1)
            rhs = jnp.concatenate([weights_out(l, i, j) for j in range(4)], axis=1)
            out[...] += lax.dot_general(lhs, rhs, NT, preferred_element_type=F32)
            return carry

        lax.fori_loop(0, 4, step, 0)

    def partial(lhs, wide, out):
        def step(i, carry):
            for j in range(4):
                v = jnp.dot(lhs[...], wide[i, j], preferred_element_type=F32).astype(BF16)
                out[0, i, j, pl.ds(0, R)] = v[:, :HALF]
                out[1, i, j, pl.ds(0, R)] = v[:, HALF:]
            return carry

        lax.fori_loop(0, 4, step, 0)

    def inner(l):
        v = s["z_in", l][...]
        inv = s["rinv", l][...]
        sigm = jax.nn.sigmoid(v)
        dz = (s["da", l][...] + s["da_in", l][...]) * sigm * (1.0 + v * (1.0 - sigm))
        mean = jnp.sum(dz * v, axis=1, keepdims=True) * (1.0 / WIDTH)
        s["tok"][...] = inv * inv * mean
        dz = dz * inv
        s["dzr"][...] = dz.astype(BF16)
        s["dzr_t"][...] = dz.T.astype(BF16)

    def back_down(l):
        g, h, w = s["h", LAYERS], s["h", l], s["wa", l]

        def step(i, carry):
            for j in range(4):
                rhs = w[i, j].reshape(2 * HALF, R)
                for r in range(0, ROWS, CHUNK):
                    rows = pl.ds(r, CHUNK)
                    du = lax.dot_general(s["dzr"][rows, :], rhs, NT, preferred_element_type=F32)
                    v = h[i, j, rows, :].astype(F32) * lanes2(s["tok"][rows, :])
                    g[i, j, rows, :] = (g[i, j, rows, :].astype(F32) + (du - v)).astype(BF16)
            return carry

        lax.fori_loop(0, 4, step, 0)

    in0, in1, in2 = (gather_in(l) for l in range(LAYERS))
    out0, out1, out2 = (gather_out(l) for l in range(LAYERS))
    go(in0, out0, in1, out1, in2, out2)

    core_send, core_recv = s["send"].at[N_SEMS - 1], s["recv"].at[N_SEMS - 1]

    def core_copy(src, dst):
        return pltpu.make_async_remote_copy(
            src_ref=src,
            dst_ref=dst,
            send_sem=core_send,
            recv_sem=core_recv,
            device_id=to_core,
            device_id_type=MESH,
        )

    def swap_hidden(i, carry):
        yy, zz = i // 4, i % 4
        for xx in range(2):
            col = pl.multiple_of(yy * 2048 + xx * 1024 + zz * 256 + other * HALF, HALF)
            core_copy(
                hidden.at[:, pl.ds(col, HALF)],
                s["h", 0].at[yy * c + zz * other, zz * c + yy * other, my_rows, pl.ds(xx * HALF, HALF)],
            ).start()
        return carry

    lax.fori_loop(0, 16, swap_hidden, 0)
    packs = send(pack, s["packs"].at[c], to_core)
    s["packs"][c] = pack[...]

    go(in0, out0, in1, out1)
    go(in0, out0, in1, out1)
    go(in0, out0, in2, out2)
    block = s["h", 0].at[:, :, my_rows]
    pltpu.make_async_copy(block, block, hidden_sem).wait()
    swapped = core_copy(block, s["h", 0].at[:, :, their_rows])
    swapped.wait_recv()
    swapped.wait_send()
    squares(0)
    sq = send(s["sq", 0], s["sq_in", 0], to_core)
    go(in0, out0, in1, out1, in2, out2)
    arrived(sq)
    inverse(0)
    go(in0)
    down(0)
    zc = send(s["z", 0], s["z_in", 0], to_core)
    go(out0, in1, out1, in2, out2)
    arrived(zc)
    activate(0)
    up(0)
    sq = send(s["sq", 1], s["sq_in", 1], to_core)
    go(in1)
    down(1)
    zc = send(s["z", 1], s["z_in", 1], to_core)
    go(out1, in2, out2)
    arrived(sq)
    inverse(1)
    arrived(zc)
    activate(1)
    up(1)
    sq = send(s["sq", 2], s["sq_in", 2], to_core)
    go(in2)
    down(2)
    zc = send(s["z", 2], s["z_in", 2], to_core)
    go(out2)
    gains()
    arrived(sq)
    inverse(2)
    arrived(zc)
    activate(2)
    up(2)
    sq = send(s["sq", 3], s["sq_in", 3], to_core)
    qc = send(s["q"], s["q_in"], to_core)
    arrived(packs, sq)
    inverse(3)
    arrived(qc)
    head()
    top()

    back_up(2)
    dc = send(s["da", 2], s["da_in", 2], to_core)
    partial(s["act_t", 2], s["h", LAYERS], s["gb", 2])
    out2 = scatter_out(2)
    go(out2)
    arrived(dc)
    inner(2)
    partial(s["dzr_t"], s["h", 2], s["ga", 2])
    in2 = scatter_in(2)
    go(in2)
    back_down(2)
    go(out2, in2)
    back_up(1)
    dc = send(s["da", 1], s["da_in", 1], to_core)
    go(out2)
    partial(s["act_t", 1], s["h", LAYERS], s["gb", 1])
    out1 = scatter_out(1)
    go(out1)
    go(out2, in2)
    arrived(dc)
    inner(1)
    partial(s["dzr_t"], s["h", 1], s["ga", 1])
    in1 = scatter_in(1)
    go(in1)
    go(out2, in2)
    back_down(1)
    go(out1, in1)
    back_up(0)
    dc = send(s["da", 0], s["da_in", 0], to_core)
    go(out2, in2, out1)
    partial(s["act_t", 0], s["h", LAYERS], s["gb", 0])
    out0 = scatter_out(0)
    go(out0)
    go(out2, in2)
    go(out1, in1)
    arrived(dc)
    inner(0)
    partial(s["dzr_t"], s["h", 0], s["ga", 0])
    in0 = scatter_in(0)
    go(in0)
    for _ in range(7):
        go(out2, in2, out1, in1, out0, in0)
    for copy in started:
        copy.wait_send()


def body(hidden, seg_ids, ranks, adapter_in, adapter_out, score_head, final_gain):
    pack = jnp.concatenate(
        [
            score_head.astype(F32)[None],
            final_gain.astype(F32)[None],
            seg_ids.astype(F32),
            jnp.pad(ranks[0].astype(F32), ((0, 0), (0, 248))),
            jnp.zeros((3, 256), F32),
        ],
        axis=0,
    )
    vmem = pl.BlockSpec(memory_space=pltpu.VMEM)
    hbm = pl.BlockSpec(memory_space=pl.ANY)
    grad_in, grad_out, grad_vec = pl.pallas_call(
        kernel,
        out_shape=(
            jax.ShapeDtypeStruct((LAYERS, 2 * HALF, R), F32),
            jax.ShapeDtypeStruct((LAYERS, R, 2 * HALF), F32),
            jax.ShapeDtypeStruct((8, 2 * HALF), F32),
        ),
        in_specs=[hbm, hbm, hbm, vmem],
        out_specs=(vmem, vmem, vmem),
        scratch_shapes=list(scratch().values()),
        compiler_params=pltpu.CompilerParams(
            collective_id=0, has_side_effects=True, vmem_limit_bytes=60 * 1024 * 1024
        ),
        name="adapters",
    )(hidden, adapter_in, adapter_out, pack)
    return grad_in, grad_out, grad_vec[0], grad_vec[1]


def solution(mesh):
    placed = (
        P(("rep", "shard"), None),
        P(("rep", "shard"), None),
        P(("rep", "shard"), None, None),
        P(None, "shard", None),
        P(None, None, "shard"),
        P("shard"),
        P("shard"),
    )
    return jax.shard_map(
        body,
        mesh=mesh,
        in_specs=placed,
        out_specs=(P(None, "shard", None), P(None, None, "shard"), P("shard"), P("shard")),
        check_vma=False,
    )
```

```python
import jax
import jax.numpy as jnp
from jax import lax
from jax.experimental import pallas as pl
from jax.experimental.pallas import tpu as pltpu
from jax.sharding import PartitionSpec as P

EPS = 1e-06
MESH = pl.DeviceIdType.MESH
F32 = jnp.float32
BF16 = jnp.bfloat16
LAYERS = 3
WIDTH = 8192
TOK = 256
ROWS = 2 * TOK
R = 128
HALF = 128
EXTRA = 16
N_SEMS = 240
NT = (((1,), (1,)), ((), ()))
CHUNK = 256


def unit_rows(layer):
    return R + EXTRA if layer == LAYERS - 1 else R


def scratch():
    shapes = {}
    for level in range(LAYERS + 1):
        shapes["h", level] = pltpu.VMEM((4, 4, ROWS, 2 * HALF), BF16)
        shapes["sq", level] = pltpu.VMEM((ROWS, 128), F32)
        shapes["sq_in", level] = pltpu.VMEM((ROWS, 128), F32)
        shapes["rinv", level] = pltpu.VMEM((ROWS, 128), F32)
    for layer in range(LAYERS):
        rows = unit_rows(layer)
        shapes["own", layer] = pltpu.VMEM((rows, HALF), BF16)
        shapes["wa", layer] = pltpu.VMEM((4, 4, 2, HALF, R), BF16)
        shapes["wb", layer] = pltpu.VMEM((2, 4, 4, rows, HALF), BF16)
        shapes["z", layer] = pltpu.VMEM((ROWS, R), F32)
        shapes["z_in", layer] = pltpu.VMEM((ROWS, R), F32)
        shapes["act_t", layer] = pltpu.VMEM((R, ROWS), BF16)
        shapes["da", layer] = pltpu.VMEM((ROWS, R), F32)
        shapes["da_in", layer] = pltpu.VMEM((ROWS, R), F32)
        shapes["ga", layer] = pltpu.VMEM((2, 4, 4, R, HALF), BF16)
        shapes["ga1", layer] = pltpu.VMEM((2, 4, R, HALF), BF16)
        shapes["ga2", layer] = pltpu.VMEM((2, 2, 4, R, HALF), BF16)
        shapes["ga3", layer] = pltpu.VMEM((2, 4, R, HALF), BF16)
        shapes["ga4", layer] = pltpu.VMEM((2, 2, R, HALF), F32)
        shapes["gb", layer] = pltpu.VMEM((2, 4, 4, rows, HALF), BF16)
        shapes["gb1", layer] = pltpu.VMEM((4, 4, rows, HALF), BF16)
        shapes["gb2", layer] = pltpu.VMEM((4, rows, HALF), BF16)
        shapes["gb3", layer] = pltpu.VMEM((2, 4, rows, HALF), BF16)
        shapes["gb4", layer] = pltpu.VMEM((3, rows, HALF), BF16)
        shapes["gb5", layer] = pltpu.VMEM((2, 2, rows, HALF), F32)
    shapes["act"] = pltpu.VMEM((ROWS, R), BF16)
    shapes["dzr"] = pltpu.VMEM((ROWS, R), BF16)
    shapes["dzr_t"] = pltpu.VMEM((R, ROWS), BF16)
    shapes["tok"] = pltpu.VMEM((ROWS, 128), F32)
    shapes["q"] = pltpu.VMEM((ROWS, 128), F32)
    shapes["q_in"] = pltpu.VMEM((ROWS, 128), F32)
    shapes["coef"] = pltpu.VMEM((ROWS, 128), F32)
    shapes["vec"] = pltpu.VMEM((16, ROWS), BF16)
    shapes["hg"] = pltpu.VMEM((4, 4, 8, 2 * HALF), F32)
    shapes["packs"] = pltpu.VMEM((2, 8, 256), F32)
    shapes["send"] = pltpu.SemaphoreType.DMA((N_SEMS,))
    shapes["recv"] = pltpu.SemaphoreType.DMA((N_SEMS,))
    shapes["local"] = pltpu.SemaphoreType.DMA((16,))
    return shapes


def kernel(
    hidden, seg_ids, ranks, w_in, w_out, score_head, final_gain,
    grad_in, grad_out, grad_head, grad_gain, *refs
):
    s = dict(zip(scratch(), refs))
    rep, shard = lax.axis_index("rep"), lax.axis_index("shard")
    xh, c = rep // 2, rep % 2
    y, xl, z = shard // 8, (shard // 4) % 2, shard % 4
    other = 1 - c
    low, high = pl.ds(0, 2), pl.ds(2, 2)
    p, q = y * other + z * c, z * other + y * c
    pp, p2, pm = (p + 1) % 4, (p + 2) % 4, (p + 3) % 4
    qp, q2, qm = (q + 1) % 4, (q + 2) % 4, (q + 3) % 4

    def device(x_by, p_by, q_by):
        x = (xh * 2 + xl + x_by) % 4
        y_to = (y + p_by * other + q_by * c) % 4
        z_to = (z + q_by * other + p_by * c) % 4
        return (x // 2 * 2 + c, y_to * 8 + x % 2 * 4 + z_to)

    to_p = [device(0, by, 0) for by in range(1, 4)]
    to_q = [device(0, 0, by) for by in range(1, 4)]
    to_xp = [device(1, 0, by) for by in range(4)]
    to_xm = [device(3, 0, by) for by in range(4)]
    to_core = (xh * 2 + other, shard)
    to_rep = ((1 - xh) * 2 + c, shard)
    to_both = ((1 - xh) * 2 + other, shard)
    to_x = to_xp[:2] + to_xm[2:]

    used = [0, 0]
    started = []

    def send(src, dst, to):
        i = used[0]
        used[0] += 1
        copy = pltpu.make_async_remote_copy(
            src_ref=src,
            dst_ref=dst,
            send_sem=s["send"].at[i],
            recv_sem=s["recv"].at[i],
            device_id=to,
            device_id_type=MESH,
        )
        copy.start()
        started.append(copy)
        return copy

    def local(src, dst):
        copy = pltpu.make_async_copy(src, dst, s["local"].at[used[1]])
        used[1] += 1
        copy.start()
        return copy

    def arrived(*copies):
        for copy in copies:
            copy.wait_recv()

    mine = pl.ds(pl.multiple_of(c * HALF, HALF), HALF)
    my_rows = pl.ds(pl.multiple_of(c * TOK, TOK), TOK)
    their_rows = pl.ds(pl.multiple_of(other * TOK, TOK), TOK)
    local_in = [
        local(w_in.at[l, mine], s["wa", l].at[p, q, xl]) for l in range(LAYERS)
    ]
    local_out = [
        local(w_out.at[l, :, mine], s["own", l].at[pl.ds(0, R)]) for l in range(LAYERS)
    ]

    def head_row():
        return score_head[...].astype(F32).reshape(1, 2 * HALF)

    def gain_row():
        return final_gain[...].astype(F32).reshape(1, 2 * HALF)

    barrier = pltpu.get_barrier_semaphore()
    partners = (*to_p, *to_q, *to_xp, *to_xm, to_core, to_rep, to_both)
    for partner in partners:
        pl.semaphore_signal(barrier, inc=1, device_id=partner, device_id_type=MESH)

    hidden_sem = s["local"].at[15]

    def load_hidden(i, carry):
        yy, zz = i // 4, i % 4
        for xx in range(2):
            col = pl.multiple_of(yy * 2048 + xx * 1024 + zz * 256 + c * HALF, HALF)
            pltpu.make_async_copy(
                hidden.at[:, pl.ds(col, HALF)],
                s["h", 0].at[yy * other + zz * c, zz * other + yy * c, my_rows, pl.ds(xx * HALF, HALF)],
                hidden_sem,
            ).start()
        return carry

    lax.fori_loop(0, 16, load_hidden, 0)
    pl.semaphore_wait(barrier, len(partners))

    def gather_in(l):
        w, src = s["wa", l], w_in.at[l, mine]
        copies = [send(src, w.at[p, q, xl], to) for to in (*to_q, *to_x)]
        yield
        local_in[l].wait()
        arrived(*copies)
        a = send(w.at[p, low], w.at[p, low], to_p[0])
        b = send(w.at[p, high], w.at[p, high], to_p[2])
        copies = [
            send(w.at[p, high], w.at[p, high], to_p[0]),
            send(w.at[p, low], w.at[p, low], to_p[2]),
        ]
        yield
        arrived(a, b)
        copies += [
            send(w.at[pm, low], w.at[pm, low], to_p[0]),
            send(w.at[pp, high], w.at[pp, high], to_p[2]),
        ]
        yield
        arrived(*copies)
        yield

    def gather_out(l):
        w, own, rows = s["wb", l], s["own", l], unit_rows(l)
        local_out[l].wait()
        if rows > R:
            both = head_row() * gain_row()
            both = both[:, :HALF] * (1 - c).astype(F32) + both[:, HALF:] * c.astype(F32)
            hi = both.astype(BF16)
            lo = (both - hi.astype(F32)).astype(BF16)
            row = lax.broadcasted_iota(jnp.int32, (EXTRA, HALF), 0)
            own[pl.ds(R, EXTRA), :] = jnp.where(
                row == 0, hi.astype(F32), jnp.where(row == 1, lo.astype(F32), 0.0)
            ).astype(BF16)
        copies = [send(own, w.at[xl, p, q], to) for to in to_p]
        kept = local(own, w.at[xl, p, q])
        yield
        kept.wait()
        arrived(*copies)
        a = send(w.at[xl, low, q], w.at[xl, low, q], to_q[0])
        b = send(w.at[xl, high, q], w.at[xl, high, q], to_q[2])
        copies = [
            send(w.at[xl, high, q], w.at[xl, high, q], to_q[0]),
            send(w.at[xl, low, q], w.at[xl, low, q], to_q[2]),
        ]
        across = [
            send(w.at[xl, low, q], w.at[xl, low, q], to_xp[0]),
            send(w.at[xl, high, q], w.at[xl, high, q], to_xm[0]),
        ]
        yield
        arrived(a, b)
        copies += [
            send(w.at[xl, low, qm], w.at[xl, low, qm], to_q[0]),
            send(w.at[xl, high, qp], w.at[xl, high, qp], to_q[2]),
        ]
        across += [
            send(w.at[xl, low, qm], w.at[xl, low, qm], to_xp[0]),
            send(w.at[xl, high, qp], w.at[xl, high, qp], to_xm[0]),
        ]
        yield
        arrived(*copies)
        across += [
            send(w.at[xl, low, qp], w.at[xl, low, qp], to_xp[0]),
            send(w.at[xl, high, qm], w.at[xl, high, qm], to_xm[0]),
            send(w.at[xl, low, q2], w.at[xl, low, q2], to_xp[0]),
            send(w.at[xl, high, q2], w.at[xl, high, q2], to_xm[0]),
        ]
        yield
        arrived(*across)
        yield

    def total(*parts):
        value = parts[0].astype(F32)
        for part in parts[1:]:
            value = value + part.astype(F32)
        return value

    def finish(own, l, store):
        copies = [send(own.at[c, xh], own.at[c, xh], to) for to in (to_rep, to_core, to_both)]
        yield
        arrived(*copies)
        for half in range(2):
            store(l, half, own[half, 0] + own[half, 1])
        yield

    def scatter_out(l):
        g = s["gb", l]
        r1, r2, r3, r4, r5 = (s["gb%d" % i, l] for i in range(1, 6))
        across = []
        for j in (q2, qp, qm, q):
            across += [
                send(g.at[1 - xl, low, j], r1.at[low, j], to_xp[0]),
                send(g.at[1 - xl, high, j], r1.at[high, j], to_xm[0]),
            ]
        yield
        arrived(*across[:2])
        for i in range(4):
            g[xl, i, q2] = total(g[xl, i, q2], r1[i, q2]).astype(BF16)
        a = send(g.at[xl, low, q2], r2.at[low], to_q[0])
        b = send(g.at[xl, high, q2], r2.at[high], to_q[2])
        yield
        arrived(*across[2:6])
        for i in range(2):
            g[xl, i + 2, qp] = total(g[xl, i + 2, qp], r1[i + 2, qp]).astype(BF16)
            g[xl, i, qm] = total(g[xl, i, qm], r1[i, qm]).astype(BF16)
        copies = [
            send(g.at[xl, high, qp], r3.at[0, high], to_q[0]),
            send(g.at[xl, low, qm], r3.at[1, low], to_q[2]),
        ]
        arrived(a, b)
        for i in range(2):
            g[xl, i, qp] = total(g[xl, i, qp], r1[i, qp], r2[i]).astype(BF16)
            g[xl, i + 2, qm] = total(g[xl, i + 2, qm], r1[i + 2, qm], r2[i + 2]).astype(BF16)
        copies += [
            send(g.at[xl, low, qp], r3.at[0, low], to_q[0]),
            send(g.at[xl, high, qm], r3.at[1, high], to_q[2]),
        ]
        yield
        arrived(*across[6:], *copies)
        for i in range(4):
            g[xl, i, q] = total(g[xl, i, q], r1[i, q], r3[0, i], r3[1, i]).astype(BF16)
        copies = [send(g.at[xl, (p + 1 + k) % 4, q], r4.at[k], to_p[k]) for k in range(3)]
        yield
        arrived(*copies)
        r5[c, xh] = total(g[xl, p, q], r4[0], r4[1], r4[2])
        yield from finish(r5, l, store_out)

    def scatter_in(l):
        g = s["ga", l]
        r1, r2, r3, r4 = (s["ga%d" % i, l] for i in range(1, 5))
        a = send(g.at[:, p2, low], r1.at[:, low], to_p[0])
        b = send(g.at[:, p2, high], r1.at[:, high], to_p[2])
        copies = [
            send(g.at[:, pp, high], r2.at[0, :, high], to_p[0]),
            send(g.at[:, pm, low], r2.at[1, :, low], to_p[2]),
        ]
        yield
        arrived(a, b)
        for x in range(2):
            for j in range(2):
                g[x, pp, j] = total(g[x, pp, j], r1[x, j]).astype(BF16)
                g[x, pm, j + 2] = total(g[x, pm, j + 2], r1[x, j + 2]).astype(BF16)
        copies += [
            send(g.at[:, pp, low], r2.at[0, :, low], to_p[0]),
            send(g.at[:, pm, high], r2.at[1, :, high], to_p[2]),
        ]
        yield
        arrived(*copies)
        for x in range(2):
            for j in range(4):
                g[x, p, j] = total(g[x, p, j], r2[0, x, j], r2[1, x, j]).astype(BF16)
        copies = [send(g.at[xl, p, (q + 1 + k) % 4], r3.at[0, k + 1], to_q[k]) for k in range(3)]
        copies += [send(g.at[1 - xl, p, (q + k) % 4], r3.at[1, k], to_x[k]) for k in range(4)]
        yield
        arrived(*copies)
        r4[c, xh] = total(
            g[xl, p, q], *[r3[0, k] for k in range(1, 4)], *[r3[1, k] for k in range(4)]
        )
        yield from finish(r4, l, store_in)

    vecs = []

    def store_in(l, half, total):
        grad_in[l, pl.ds(half * HALF, HALF), :] = total.T

    def store_out(l, half, total):
        lanes = pl.ds(half * HALF, HALF)
        grad_out[l, :, lanes] = total[:R]
        if unit_rows(l) > R:
            vec = total[R : R + 8]
            row = lax.broadcasted_iota(jnp.int32, (8, HALF), 0)
            vec = jnp.sum(jnp.where(row == 0, vec, 0.0), axis=0, keepdims=True)
            vecs.append(vec)
            if half == 1:
                vec = jnp.concatenate(vecs, axis=1)
                grad_head[...] = (vec * gain_row()).reshape(2 * HALF)
                grad_gain[...] = (vec * head_row()).reshape(2 * HALF)

    def go(*jobs):
        for job in jobs:
            next(job, None)

    def lanes2(values):
        return jnp.concatenate([values, values], axis=1)

    def weights_out(l, i, j):
        w = s["wb", l]
        return jnp.concatenate([w[0, i, j, pl.ds(0, R)], w[1, i, j, pl.ds(0, R)]], axis=1)

    def squares(level):
        h, out = s["h", level], s["sq", level]
        out[...] = jnp.zeros_like(out)

        def step(i, carry):
            for r in range(0, ROWS, CHUNK):
                rows = pl.ds(r, CHUNK)
                total = out[rows, :]
                for j in range(4):
                    v = h[i, j, rows, :].astype(F32)
                    v = v * v
                    total = total + (v[:, :128] + v[:, 128:])
                out[rows, :] = total
            return carry

        lax.fori_loop(0, 4, step, 0)

    def down(l):
        h, w, out = s["h", l], s["wa", l], s["z", l]
        out[...] = jnp.zeros_like(out)

        def step(i, carry):
            lhs = jnp.concatenate([h[i, j] for j in range(4)], axis=1)
            out[...] += jnp.dot(lhs, w[i].reshape(4 * 2 * HALF, R), preferred_element_type=F32)
            return carry

        lax.fori_loop(0, 4, step, 0)

    def inverse(level):
        total = jnp.sum(s["sq", level][...] + s["sq_in", level][...], axis=1, keepdims=True)
        inv = lax.rsqrt(total * (1.0 / WIDTH) + EPS)
        s["rinv", level][...] = jnp.broadcast_to(inv, (ROWS, 128))

    def activate(l):
        v = (s["z", l][...] + s["z_in", l][...]) * s["rinv", l][...]
        s["z_in", l][...] = v
        active = v * jax.nn.sigmoid(v)
        s["act"][...] = active.astype(BF16)
        s["act_t", l][...] = active.T.astype(BF16)

    def up(l):
        h, out, sq = s["h", l], s["h", l + 1], s["sq", l + 1]
        last = l == LAYERS - 1
        sq[...] = jnp.zeros_like(sq)
        if last:
            s["q"][...] = jnp.zeros_like(s["q"])

        def step(i, carry):
            for j in range(4):
                w = weights_out(l, i, j)
                if last:
                    hg = s["hg"][i, j, 0:1, :]
                for r in range(0, ROWS, CHUNK):
                    rows = pl.ds(r, CHUNK)
                    v = jnp.dot(s["act"][rows, :], w, preferred_element_type=F32)
                    v = (h[i, j, rows, :].astype(F32) + v).astype(BF16)
                    out[i, j, rows, :] = v
                    v = v.astype(F32)
                    if last:
                        t = v * hg
                        s["q"][rows, :] += t[:, :128] + t[:, 128:]
                    v = v * v
                    sq[rows, :] += v[:, :128] + v[:, 128:]
            return carry

        lax.fori_loop(0, 4, step, 0)

    def gains():
        w = s["wb", LAYERS - 1]

        def step(i, carry):
            for j in range(4):
                for x in range(2):
                    rows = w[x, i, j, pl.ds(R, EXTRA)].astype(F32)
                    both = jnp.sum(rows, axis=0, keepdims=True)
                    s["hg"][i, j, :, pl.ds(x * HALF, HALF)] = jnp.broadcast_to(both, (8, HALF))
            return carry

        lax.fori_loop(0, 4, step, 0)

    def head():
        inv = s["rinv", LAYERS][...]
        dot_q = jnp.sum(s["q"][...] + s["q_in"][...], axis=1, keepdims=True)
        n_q = dot_q * inv
        seg_row = lax.broadcasted_iota(jnp.int32, (16, TOK), 0).astype(F32)
        onehots, rewards, counts = [], [], []
        for core in range(2):
            onehot = (s["packs"][core, 2:3, :] == seg_row).astype(F32)
            count = jnp.sum(onehot, axis=1, keepdims=True)
            total = jnp.dot(
                onehot,
                n_q[core * TOK : (core + 1) * TOK],
                precision=lax.Precision.HIGHEST,
                preferred_element_type=F32,
            )
            onehots.append(onehot)
            counts.append(count)
            rewards.append(total / count)
        place = lax.broadcasted_iota(jnp.int32, (8, 128), 0)
        lane = lax.broadcasted_iota(jnp.int32, (8, 128), 1)
        real = lane < 8
        for core in range(2):
            d_reward = []
            for k in range(2):
                order = s["packs"][core, 3 + k : 4 + k, 0:128]
                chosen = jnp.where(real & (order == place.astype(F32)), 1.0, 0.0)
                reward = rewards[core][8 * k : 8 * k + 8]
                placed = jnp.sum(chosen * reward, axis=0, keepdims=True)
                expo = jnp.exp(placed)
                suffix = jnp.sum(
                    jnp.where(real & (lane >= place), expo, 0.0), axis=1, keepdims=True
                )
                prefix = jnp.sum(
                    jnp.where(place <= lane, 1.0 / suffix, 0.0), axis=0, keepdims=True
                )
                d_placed = -1.0 + expo * prefix
                d_reward.append(
                    jnp.sum(jnp.where(chosen > 0.0, d_placed, 0.0), axis=1, keepdims=True)
                )
            scaled = jnp.concatenate(d_reward, axis=0) / counts[core]
            coef = lax.dot_general(
                onehots[core],
                jnp.broadcast_to(scaled, (16, 128)),
                (((0,), (0,)), ((), ())),
                precision=lax.Precision.HIGHEST,
                preferred_element_type=F32,
            )
            rows = pl.ds(core * TOK, TOK)
            inv_c = inv[core * TOK : (core + 1) * TOK]
            first = coef * inv_c
            s["coef"][rows, :] = first
            s["tok"][rows, :] = (
                first * inv_c * inv_c * dot_q[core * TOK : (core + 1) * TOK] * (1.0 / WIDTH)
            )
        vec = s["coef"][...].T[:8]
        hi = vec.astype(BF16)
        lo = (vec - hi.astype(F32)).astype(BF16)
        s["vec"][...] = jnp.concatenate([hi.astype(F32), lo.astype(F32)], axis=0).astype(BF16)

    def top():
        h, g = s["h", LAYERS], s["gb", LAYERS - 1]

        def step(i, carry):
            row = lax.broadcasted_iota(jnp.int32, (EXTRA, 256), 0)
            for j in range(4):
                vec = jnp.dot(s["vec"][...], h[i, j], preferred_element_type=F32)
                vec = jnp.where(row == 0, vec[:8][0:1] + vec[8:][0:1], 0.0).astype(BF16)
                g[0, i, j, pl.ds(R, EXTRA)] = vec[:, :HALF]
                g[1, i, j, pl.ds(R, EXTRA)] = vec[:, HALF:]
                hg = s["hg"][i, j, 0:1, :]
                for r in range(0, ROWS, CHUNK):
                    rows = pl.ds(r, CHUNK)
                    v = h[i, j, rows, :].astype(F32)
                    v = lanes2(s["coef"][rows, :]) * hg - v * lanes2(s["tok"][rows, :])
                    h[i, j, rows, :] = v.astype(BF16)
            return carry

        lax.fori_loop(0, 4, step, 0)

    def back_up(l):
        g, out = s["h", LAYERS], s["da", l]
        out[...] = jnp.zeros_like(out)

        def step(i, carry):
            lhs = jnp.concatenate([g[i, j] for j in range(4)], axis=1)
            rhs = jnp.concatenate([weights_out(l, i, j) for j in range(4)], axis=1)
            out[...] += lax.dot_general(lhs, rhs, NT, preferred_element_type=F32)
            return carry

        lax.fori_loop(0, 4, step, 0)

    def partial(lhs, wide, out):
        def step(i, carry):
            for j in range(4):
                v = jnp.dot(lhs[...], wide[i, j], preferred_element_type=F32).astype(BF16)
                out[0, i, j, pl.ds(0, R)] = v[:, :HALF]
                out[1, i, j, pl.ds(0, R)] = v[:, HALF:]
            return carry

        lax.fori_loop(0, 4, step, 0)

    def inner(l):
        v = s["z_in", l][...]
        inv = s["rinv", l][...]
        sigm = jax.nn.sigmoid(v)
        dz = (s["da", l][...] + s["da_in", l][...]) * sigm * (1.0 + v * (1.0 - sigm))
        mean = jnp.sum(dz * v, axis=1, keepdims=True) * (1.0 / WIDTH)
        s["tok"][...] = inv * inv * mean
        dz = dz * inv
        s["dzr"][...] = dz.astype(BF16)
        s["dzr_t"][...] = dz.T.astype(BF16)

    def back_down(l):
        g, h, w = s["h", LAYERS], s["h", l], s["wa", l]

        def step(i, carry):
            for j in range(4):
                rhs = w[i, j].reshape(2 * HALF, R)
                for r in range(0, ROWS, CHUNK):
                    rows = pl.ds(r, CHUNK)
                    du = lax.dot_general(s["dzr"][rows, :], rhs, NT, preferred_element_type=F32)
                    v = h[i, j, rows, :].astype(F32) * lanes2(s["tok"][rows, :])
                    g[i, j, rows, :] = (g[i, j, rows, :].astype(F32) + (du - v)).astype(BF16)
            return carry

        lax.fori_loop(0, 4, step, 0)

    in0, in1, in2 = (gather_in(l) for l in range(LAYERS))
    out0, out1, out2 = (gather_out(l) for l in range(LAYERS))
    go(in0, out0)

    core_send, core_recv = s["send"].at[N_SEMS - 1], s["recv"].at[N_SEMS - 1]

    def core_copy(src, dst):
        return pltpu.make_async_remote_copy(
            src_ref=src,
            dst_ref=dst,
            send_sem=core_send,
            recv_sem=core_recv,
            device_id=to_core,
            device_id_type=MESH,
        )

    def swap_hidden(i, carry):
        yy, zz = i // 4, i % 4
        for xx in range(2):
            col = pl.multiple_of(yy * 2048 + xx * 1024 + zz * 256 + other * HALF, HALF)
            core_copy(
                hidden.at[:, pl.ds(col, HALF)],
                s["h", 0].at[yy * c + zz * other, zz * c + yy * other, my_rows, pl.ds(xx * HALF, HALF)],
            ).start()
        return carry

    lax.fori_loop(0, 16, swap_hidden, 0)
    s["packs"][c, 2:3, :] = seg_ids[...].astype(F32)
    s["packs"][c, 3:5, 0:8] = ranks[0].astype(F32)
    packs = send(s["packs"].at[c], s["packs"].at[c], to_core)

    go(in1, out1, in2, out2)
    go(in0, out0, in1, out1, in2, out2)
    block = s["h", 0].at[:, :, my_rows]
    pltpu.make_async_copy(block, block, hidden_sem).wait()
    swapped = core_copy(block, s["h", 0].at[:, :, their_rows])
    swapped.wait_recv()
    swapped.wait_send()
    squares(0)
    sq = send(s["sq", 0], s["sq_in", 0], to_core)
    go(in0, out0, in1, out1)
    arrived(sq)
    inverse(0)
    go(out0, in0)
    down(0)
    zc = send(s["z", 0], s["z_in", 0], to_core)
    go(out1, in2, out2)
    arrived(zc)
    activate(0)
    go(out0)
    up(0)
    sq = send(s["sq", 1], s["sq_in", 1], to_core)
    go(in1, out2)
    down(1)
    zc = send(s["z", 1], s["z_in", 1], to_core)
    arrived(sq)
    inverse(1)
    arrived(zc)
    activate(1)
    go(out1)
    up(1)
    sq = send(s["sq", 2], s["sq_in", 2], to_core)
    go(in2)
    down(2)
    zc = send(s["z", 2], s["z_in", 2], to_core)
    arrived(sq)
    inverse(2)
    go(out2)
    gains()
    arrived(zc)
    activate(2)
    up(2)
    sq = send(s["sq", 3], s["sq_in", 3], to_core)
    qc = send(s["q"], s["q_in"], to_core)
    arrived(packs, sq)
    inverse(3)
    arrived(qc)
    head()
    top()

    back_up(2)
    dc = send(s["da", 2], s["da_in", 2], to_core)
    partial(s["act_t", 2], s["h", LAYERS], s["gb", 2])
    out2 = scatter_out(2)
    go(out2)
    arrived(dc)
    inner(2)
    partial(s["dzr_t"], s["h", 2], s["ga", 2])
    in2 = scatter_in(2)
    go(in2)
    back_down(2)
    go(out2)
    back_up(1)
    dc = send(s["da", 1], s["da_in", 1], to_core)
    partial(s["act_t", 1], s["h", LAYERS], s["gb", 1])
    out1 = scatter_out(1)
    go(out1, in2, out2)
    arrived(dc)
    inner(1)
    partial(s["dzr_t"], s["h", 1], s["ga", 1])
    in1 = scatter_in(1)
    go(in1, out1)
    back_down(1)
    go(in2, out2)
    back_up(0)
    dc = send(s["da", 0], s["da_in", 0], to_core)
    partial(s["act_t", 0], s["h", LAYERS], s["gb", 0])
    out0 = scatter_out(0)
    go(out0, in1, out1)
    arrived(dc)
    inner(0)
    partial(s["dzr_t"], s["h", 0], s["ga", 0])
    in0 = scatter_in(0)
    go(in0, out0, in2, out2, in1, out1)
    go(in0, out0, in2, out2, in1, out1)
    go(in0, out0, in1, out1)
    go(in0, out0)
    go(in0, out0)
    for copy in started:
        copy.wait_send()


def deliver(*refs):
    for i in range(4):
        refs[i + 4][...] = refs[i][...]


def body(hidden, seg_ids, ranks, adapter_in, adapter_out, score_head, final_gain):
    vmem = pl.BlockSpec(memory_space=pltpu.VMEM)
    hbm = pl.BlockSpec(memory_space=pl.ANY)
    shapes = (
        jax.ShapeDtypeStruct((LAYERS, 2 * HALF, R), F32),
        jax.ShapeDtypeStruct((LAYERS, R, 2 * HALF), F32),
        jax.ShapeDtypeStruct((2 * HALF,), F32),
        jax.ShapeDtypeStruct((2 * HALF,), F32),
    )
    grads = pl.pallas_call(
        kernel,
        out_shape=shapes,
        in_specs=[hbm, vmem, vmem, hbm, hbm, vmem, vmem],
        out_specs=(vmem,) * 4,
        scratch_shapes=list(scratch().values()),
        compiler_params=pltpu.CompilerParams(
            collective_id=0, has_side_effects=True, vmem_limit_bytes=60 * 1024 * 1024
        ),
        name="adapters",
    )(hidden, seg_ids, ranks, adapter_in, adapter_out, score_head, final_gain)
    return pl.pallas_call(
        deliver,
        out_shape=shapes,
        in_specs=[vmem] * 4,
        out_specs=(vmem,) * 4,
        name="deliver",
    )(*grads)


def solution(mesh):
    placed = (
        P(("rep", "shard"), None),
        P(("rep", "shard"), None),
        P(("rep", "shard"), None, None),
        P(None, "shard", None),
        P(None, None, "shard"),
        P("shard"),
        P("shard"),
    )
    return jax.shard_map(
        body,
        mesh=mesh,
        in_specs=placed,
        out_specs=(P(None, "shard", None), P(None, None, "shard"), P("shard"), P("shard")),
        check_vma=False,
    )
```

```python
import jax
import jax.numpy as jnp
from jax import lax
from jax.experimental import pallas as pl
from jax.experimental.pallas import tpu as pltpu
from jax.sharding import PartitionSpec as P

EPS = 1e-06
MESH = pl.DeviceIdType.MESH
F32 = jnp.float32
BF16 = jnp.bfloat16
LAYERS = 3
WIDTH = 8192
TOK = 256
ROWS = 2 * TOK
R = 128
HALF = 128
EXTRA = 16
N_SEMS = 240
NT = (((1,), (1,)), ((), ()))
CHUNK = 256

def unit_rows(layer):
    return R + EXTRA if layer == LAYERS - 1 else R

def scratch():
    shapes = {}
    for level in range(LAYERS + 1):
        shapes["h", level] = pltpu.VMEM((4, 4, ROWS, 2 * HALF), BF16)
        shapes["sq", level] = pltpu.VMEM((ROWS, 128), F32)
        shapes["sq_in", level] = pltpu.VMEM((ROWS, 128), F32)
        shapes["rinv", level] = pltpu.VMEM((ROWS, 128), F32)
    for layer in range(LAYERS):
        rows = unit_rows(layer)
        shapes["own", layer] = pltpu.VMEM((rows, HALF), BF16)
        shapes["wa", layer] = pltpu.VMEM((4, 4, 2, HALF, R), BF16)
        shapes["wb", layer] = pltpu.VMEM((2, 4, 4, rows, HALF), BF16)
        shapes["z", layer] = pltpu.VMEM((ROWS, R), F32)
        shapes["z_in", layer] = pltpu.VMEM((ROWS, R), F32)
        shapes["act_t", layer] = pltpu.VMEM((R, ROWS), BF16)
        shapes["da", layer] = pltpu.VMEM((ROWS, R), F32)
        shapes["da_in", layer] = pltpu.VMEM((ROWS, R), F32)
        shapes["ga", layer] = pltpu.VMEM((2, 4, 4, R, HALF), BF16)
        shapes["ga1", layer] = pltpu.VMEM((2, 4, R, HALF), BF16)
        shapes["ga2", layer] = pltpu.VMEM((2, 2, 4, R, HALF), BF16)
        shapes["ga3", layer] = pltpu.VMEM((2, 4, R, HALF), BF16)
        shapes["ga4", layer] = pltpu.VMEM((2, R, HALF), BF16)
        shapes["ga5", layer] = pltpu.VMEM((2, R, HALF), F32)
        shapes["gb", layer] = pltpu.VMEM((2, 4, 4, rows, HALF), BF16)
        shapes["gb1", layer] = pltpu.VMEM((4, 4, rows, HALF), BF16)
        shapes["gb2", layer] = pltpu.VMEM((4, rows, HALF), BF16)
        shapes["gb3", layer] = pltpu.VMEM((2, 4, rows, HALF), BF16)
        shapes["gb4", layer] = pltpu.VMEM((3, rows, HALF), BF16)
        shapes["gb5", layer] = pltpu.VMEM((2, rows, HALF), BF16)
        shapes["gb6", layer] = pltpu.VMEM((2, rows, HALF), F32)
    shapes["act"] = pltpu.VMEM((ROWS, R), BF16)
    shapes["dzr"] = pltpu.VMEM((ROWS, R), BF16)
    shapes["dzr_t"] = pltpu.VMEM((R, ROWS), BF16)
    shapes["tok"] = pltpu.VMEM((ROWS, 128), F32)
    shapes["q"] = pltpu.VMEM((ROWS, 128), F32)
    shapes["q_in"] = pltpu.VMEM((ROWS, 128), F32)
    shapes["coef"] = pltpu.VMEM((ROWS, 128), F32)
    shapes["vec"] = pltpu.VMEM((16, ROWS), BF16)
    shapes["hg"] = pltpu.VMEM((4, 4, 8, 2 * HALF), F32)
    shapes["seg"] = pltpu.VMEM((1, TOK), jnp.int32)
    shapes["ranks"] = pltpu.VMEM((1, 2, 8), jnp.int32)
    shapes["score"] = pltpu.VMEM((2 * HALF,), BF16)
    shapes["gain"] = pltpu.VMEM((2 * HALF,), BF16)
    shapes["out_in"] = pltpu.VMEM((LAYERS, 2 * HALF, R), F32)
    shapes["out_out"] = pltpu.VMEM((LAYERS, R, 2 * HALF), F32)
    shapes["out_head"] = pltpu.VMEM((2 * HALF,), F32)
    shapes["out_gain"] = pltpu.VMEM((2 * HALF,), F32)
    shapes["packs"] = pltpu.VMEM((2, 8, 256), F32)
    shapes["send"] = pltpu.SemaphoreType.DMA((N_SEMS,))
    shapes["recv"] = pltpu.SemaphoreType.DMA((N_SEMS,))
    shapes["local"] = pltpu.SemaphoreType.DMA((32,))
    return shapes

def kernel(
    hidden, seg_ids, ranks, w_in, w_out, score_head, final_gain,
    grad_in, grad_out, grad_head, grad_gain, *refs
):
    s = dict(zip(scratch(), refs))
    rep, shard = lax.axis_index("rep"), lax.axis_index("shard")
    xh, c = rep // 2, rep % 2
    y, xl, z = shard // 8, (shard // 4) % 2, shard % 4
    other = 1 - c
    low, high = pl.ds(0, 2), pl.ds(2, 2)
    p, q = y * other + z * c, z * other + y * c
    pp, p2, pm = (p + 1) % 4, (p + 2) % 4, (p + 3) % 4
    qp, q2, qm = (q + 1) % 4, (q + 2) % 4, (q + 3) % 4

    def device(x_by, p_by, q_by):
        x = (xh * 2 + xl + x_by) % 4
        y_to = (y + p_by * other + q_by * c) % 4
        z_to = (z + q_by * other + p_by * c) % 4
        return (x // 2 * 2 + c, y_to * 8 + x % 2 * 4 + z_to)

    to_p = [device(0, by, 0) for by in range(1, 4)]
    to_q = [device(0, 0, by) for by in range(1, 4)]
    to_xp = [device(1, 0, by) for by in range(4)]
    to_xm = [device(3, 0, by) for by in range(4)]
    to_core = (xh * 2 + other, shard)
    to_rep = ((1 - xh) * 2 + c, shard)
    to_x = to_xp[:2] + to_xm[2:]

    used = [0, 0]
    started = []

    def send(src, dst, to):
        i = used[0]
        used[0] += 1
        copy = pltpu.make_async_remote_copy(
            src_ref=src,
            dst_ref=dst,
            send_sem=s["send"].at[i],
            recv_sem=s["recv"].at[i],
            device_id=to,
            device_id_type=MESH,
        )
        copy.start()
        started.append(copy)
        return copy

    def local(src, dst):
        copy = pltpu.make_async_copy(src, dst, s["local"].at[used[1]])
        used[1] += 1
        copy.start()
        return copy

    def arrived(*copies):
        for copy in copies:
            copy.wait_recv()

    mine = pl.ds(pl.multiple_of(c * HALF, HALF), HALF)
    my_rows = pl.ds(pl.multiple_of(c * TOK, TOK), TOK)
    their_rows = pl.ds(pl.multiple_of(other * TOK, TOK), TOK)
    def head_row():
        return s["score"][...].astype(F32).reshape(1, 2 * HALF)

    def gain_row():
        return s["gain"][...].astype(F32).reshape(1, 2 * HALF)

    barrier = pltpu.get_barrier_semaphore()
    partners = (*to_p, *to_q, *to_xp, *to_xm, to_core, to_rep)
    for partner in partners:
        pl.semaphore_signal(barrier, inc=1, device_id=partner, device_id_type=MESH)

    local_in = [
        local(w_in.at[l, mine], s["wa", l].at[p, q, xl]) for l in range(LAYERS)
    ]
    local_out = [
        local(w_out.at[l, :, mine], s["own", l].at[pl.ds(0, R)]) for l in range(LAYERS)
    ]
    local_small = [
        local(src, s[name])
        for src, name in (
            (seg_ids, "seg"),
            (ranks, "ranks"),
            (score_head, "score"),
            (final_gain, "gain"),
        )
    ]

    hidden_sem = s["local"].at[31]

    def load_hidden(i, carry):
        yy, zz = i // 4, i % 4
        for xx in range(2):
            col = pl.multiple_of(yy * 2048 + xx * 1024 + zz * 256 + c * HALF, HALF)
            pltpu.make_async_copy(
                hidden.at[:, pl.ds(col, HALF)],
                s["h", 0].at[yy * other + zz * c, zz * other + yy * c, my_rows, pl.ds(xx * HALF, HALF)],
                hidden_sem,
            ).start()
        return carry

    lax.fori_loop(0, 16, load_hidden, 0)
    pl.semaphore_wait(barrier, len(partners))

    def gather_in(l):
        w, src = s["wa", l], w_in.at[l, mine]
        copies = [send(src, w.at[p, q, xl], to) for to in (*to_q, *to_x)]
        yield
        local_in[l].wait()
        arrived(*copies)
        a = send(w.at[p, low], w.at[p, low], to_p[0])
        b = send(w.at[p, high], w.at[p, high], to_p[2])
        copies = [
            send(w.at[p, high], w.at[p, high], to_p[0]),
            send(w.at[p, low], w.at[p, low], to_p[2]),
        ]
        yield
        arrived(a, b)
        copies += [
            send(w.at[pm, low], w.at[pm, low], to_p[0]),
            send(w.at[pp, high], w.at[pp, high], to_p[2]),
        ]
        yield
        arrived(*copies)
        yield

    def gather_out(l):
        w, own, rows = s["wb", l], s["own", l], unit_rows(l)
        local_out[l].wait()
        if rows > R:
            both = head_row() * gain_row()
            both = both[:, :HALF] * (1 - c).astype(F32) + both[:, HALF:] * c.astype(F32)
            hi = both.astype(BF16)
            lo = (both - hi.astype(F32)).astype(BF16)
            row = lax.broadcasted_iota(jnp.int32, (EXTRA, HALF), 0)
            own[pl.ds(R, EXTRA), :] = jnp.where(
                row == 0, hi.astype(F32), jnp.where(row == 1, lo.astype(F32), 0.0)
            ).astype(BF16)
        copies = [send(own, w.at[xl, p, q], to) for to in to_p]
        kept = local(own, w.at[xl, p, q])
        yield
        kept.wait()
        arrived(*copies)
        a = send(w.at[xl, low, q], w.at[xl, low, q], to_q[0])
        b = send(w.at[xl, high, q], w.at[xl, high, q], to_q[2])
        copies = [
            send(w.at[xl, high, q], w.at[xl, high, q], to_q[0]),
            send(w.at[xl, low, q], w.at[xl, low, q], to_q[2]),
        ]
        across = [
            send(w.at[xl, low, q], w.at[xl, low, q], to_xp[0]),
            send(w.at[xl, high, q], w.at[xl, high, q], to_xm[0]),
        ]
        yield
        arrived(a, b)
        copies += [
            send(w.at[xl, low, qm], w.at[xl, low, qm], to_q[0]),
            send(w.at[xl, high, qp], w.at[xl, high, qp], to_q[2]),
        ]
        across += [
            send(w.at[xl, low, qm], w.at[xl, low, qm], to_xp[0]),
            send(w.at[xl, high, qp], w.at[xl, high, qp], to_xm[0]),
        ]
        yield
        arrived(*copies)
        across += [
            send(w.at[xl, low, qp], w.at[xl, low, qp], to_xp[0]),
            send(w.at[xl, high, qm], w.at[xl, high, qm], to_xm[0]),
            send(w.at[xl, low, q2], w.at[xl, low, q2], to_xp[0]),
            send(w.at[xl, high, q2], w.at[xl, high, q2], to_xm[0]),
        ]
        yield
        arrived(*across)
        yield

    def total(*parts):
        value = parts[0].astype(F32)
        for part in parts[1:]:
            value = value + part.astype(F32)
        return value

    def finish(own, whole, l, store):
        copy = send(own.at[xh], own.at[xh], to_rep)
        yield
        arrived(copy)
        whole[c] = total(own[0], own[1])
        copy = send(whole.at[c], whole.at[c], to_core)
        yield
        arrived(copy)
        for half in range(2):
            store(l, half, whole[half])
        yield

    def scatter_out(l):
        g = s["gb", l]
        r1, r2, r3, r4, r5, r6 = (s["gb%d" % i, l] for i in range(1, 7))
        across = []
        for j in (q2, qp, qm, q):
            if l == LAYERS - 1:
                top(j)
            partial(s["act_t", l], s["h", LAYERS], g, [(i, j) for i in range(4)])
            across += [
                send(g.at[1 - xl, low, j], r1.at[low, j], to_xp[0]),
                send(g.at[1 - xl, high, j], r1.at[high, j], to_xm[0]),
            ]
        yield
        arrived(*across[:2])
        for i in range(4):
            g[xl, i, q2] = total(g[xl, i, q2], r1[i, q2]).astype(BF16)
        a = send(g.at[xl, low, q2], r2.at[low], to_q[0])
        b = send(g.at[xl, high, q2], r2.at[high], to_q[2])
        yield
        arrived(*across[2:6])
        for i in range(2):
            g[xl, i + 2, qp] = total(g[xl, i + 2, qp], r1[i + 2, qp]).astype(BF16)
            g[xl, i, qm] = total(g[xl, i, qm], r1[i, qm]).astype(BF16)
        copies = [
            send(g.at[xl, high, qp], r3.at[0, high], to_q[0]),
            send(g.at[xl, low, qm], r3.at[1, low], to_q[2]),
        ]
        arrived(a, b)
        for i in range(2):
            g[xl, i, qp] = total(g[xl, i, qp], r1[i, qp], r2[i]).astype(BF16)
            g[xl, i + 2, qm] = total(g[xl, i + 2, qm], r1[i + 2, qm], r2[i + 2]).astype(BF16)
        copies += [
            send(g.at[xl, low, qp], r3.at[0, low], to_q[0]),
            send(g.at[xl, high, qm], r3.at[1, high], to_q[2]),
        ]
        yield
        arrived(*across[6:], *copies)
        for i in range(4):
            g[xl, i, q] = total(g[xl, i, q], r1[i, q], r3[0, i], r3[1, i]).astype(BF16)
        copies = [send(g.at[xl, (p + 1 + k) % 4, q], r4.at[k], to_p[k]) for k in range(3)]
        yield
        arrived(*copies)
        r5[xh] = total(g[xl, p, q], r4[0], r4[1], r4[2]).astype(BF16)
        yield from finish(r5, r6, l, store_out)

    def scatter_in(l):
        g = s["ga", l]
        r1, r2, r3, r4, r5 = (s["ga%d" % i, l] for i in range(1, 6))
        partial(s["dzr_t"], s["h", l], g, [(p2, j) for j in range(4)])
        a = send(g.at[:, p2, low], r1.at[:, low], to_p[0])
        b = send(g.at[:, p2, high], r1.at[:, high], to_p[2])
        partial(s["dzr_t"], s["h", l], g, [(pp, j) for j in (2, 3)] + [(pm, j) for j in (0, 1)])
        copies = [
            send(g.at[:, pp, high], r2.at[0, :, high], to_p[0]),
            send(g.at[:, pm, low], r2.at[1, :, low], to_p[2]),
        ]
        partial(s["dzr_t"], s["h", l], g, [(pp, j) for j in (0, 1)] + [(pm, j) for j in (2, 3)])
        partial(s["dzr_t"], s["h", l], g, [(p, j) for j in range(4)])
        yield
        arrived(a, b)
        for x in range(2):
            for j in range(2):
                g[x, pp, j] = total(g[x, pp, j], r1[x, j]).astype(BF16)
                g[x, pm, j + 2] = total(g[x, pm, j + 2], r1[x, j + 2]).astype(BF16)
        copies += [
            send(g.at[:, pp, low], r2.at[0, :, low], to_p[0]),
            send(g.at[:, pm, high], r2.at[1, :, high], to_p[2]),
        ]
        yield
        arrived(*copies)
        for x in range(2):
            for j in range(4):
                g[x, p, j] = total(g[x, p, j], r2[0, x, j], r2[1, x, j]).astype(BF16)
        copies = [send(g.at[xl, p, (q + 1 + k) % 4], r3.at[0, k + 1], to_q[k]) for k in range(3)]
        copies += [send(g.at[1 - xl, p, (q + k) % 4], r3.at[1, k], to_x[k]) for k in range(4)]
        yield
        arrived(*copies)
        r4[xh] = total(
            g[xl, p, q], *[r3[0, k] for k in range(1, 4)], *[r3[1, k] for k in range(4)]
        ).astype(BF16)
        yield from finish(r4, r5, l, store_in)

    vecs, leaving = [], []

    def store_in(l, half, total):
        s["out_in"][l, pl.ds(half * HALF, HALF), :] = total.T
        if half == 1:
            leaving.append(local(s["out_in"].at[l], grad_in.at[l]))

    def store_out(l, half, total):
        lanes = pl.ds(half * HALF, HALF)
        s["out_out"][l, :, lanes] = total[:R]
        if half == 1:
            leaving.append(local(s["out_out"].at[l], grad_out.at[l]))
        if unit_rows(l) > R:
            vec = total[R : R + 8]
            row = lax.broadcasted_iota(jnp.int32, (8, HALF), 0)
            vec = jnp.sum(jnp.where(row == 0, vec, 0.0), axis=0, keepdims=True)
            vecs.append(vec)
            if half == 1:
                vec = jnp.concatenate(vecs, axis=1)
                s["out_head"][...] = (vec * gain_row()).reshape(2 * HALF)
                s["out_gain"][...] = (vec * head_row()).reshape(2 * HALF)
                leaving.append(local(s["out_head"], grad_head))
                leaving.append(local(s["out_gain"], grad_gain))

    def go(*jobs):
        for job in jobs:
            next(job, None)

    def lanes2(values):
        return jnp.concatenate([values, values], axis=1)

    def weights_out(l, i, j):
        w = s["wb", l]
        return jnp.concatenate([w[0, i, j, pl.ds(0, R)], w[1, i, j, pl.ds(0, R)]], axis=1)

    def squares(level):
        h, out = s["h", level], s["sq", level]
        out[...] = jnp.zeros_like(out)

        def step(i, carry):
            for r in range(0, ROWS, CHUNK):
                rows = pl.ds(r, CHUNK)
                total = out[rows, :]
                for j in range(4):
                    v = h[i, j, rows, :].astype(F32)
                    v = v * v
                    total = total + (v[:, :128] + v[:, 128:])
                out[rows, :] = total
            return carry

        lax.fori_loop(0, 4, step, 0)

    def down(l):
        h, w, out = s["h", l], s["wa", l], s["z", l]
        out[...] = jnp.zeros_like(out)

        def step(i, carry):
            lhs = jnp.concatenate([h[i, j] for j in range(4)], axis=1)
            out[...] += jnp.dot(lhs, w[i].reshape(4 * 2 * HALF, R), preferred_element_type=F32)
            return carry

        lax.fori_loop(0, 4, step, 0)

    def inverse(level):
        total = jnp.sum(s["sq", level][...] + s["sq_in", level][...], axis=1, keepdims=True)
        inv = lax.rsqrt(total * (1.0 / WIDTH) + EPS)
        s["rinv", level][...] = jnp.broadcast_to(inv, (ROWS, 128))

    def activate(l):
        v = (s["z", l][...] + s["z_in", l][...]) * s["rinv", l][...]
        s["z_in", l][...] = v
        active = v * jax.nn.sigmoid(v)
        s["act"][...] = active.astype(BF16)
        s["act_t", l][...] = active.T.astype(BF16)

    def up(l):
        h, out, sq = s["h", l], s["h", l + 1], s["sq", l + 1]
        last = l == LAYERS - 1
        sq[...] = jnp.zeros_like(sq)
        if last:
            s["q"][...] = jnp.zeros_like(s["q"])

        def step(i, carry):
            for j in range(4):
                w = weights_out(l, i, j)
                if last:
                    hg = s["hg"][i, j, 0:1, :]
                for r in range(0, ROWS, CHUNK):
                    rows = pl.ds(r, CHUNK)
                    v = jnp.dot(s["act"][rows, :], w, preferred_element_type=F32)
                    v = (h[i, j, rows, :].astype(F32) + v).astype(BF16)
                    out[i, j, rows, :] = v
                    v = v.astype(F32)
                    if last:
                        t = v * hg
                        s["q"][rows, :] += t[:, :128] + t[:, 128:]
                    v = v * v
                    sq[rows, :] += v[:, :128] + v[:, 128:]
            return carry

        lax.fori_loop(0, 4, step, 0)

    def gains():
        w = s["wb", LAYERS - 1]

        def step(i, carry):
            for j in range(4):
                for x in range(2):
                    rows = w[x, i, j, pl.ds(R, EXTRA)].astype(F32)
                    both = jnp.sum(rows, axis=0, keepdims=True)
                    s["hg"][i, j, :, pl.ds(x * HALF, HALF)] = jnp.broadcast_to(both, (8, HALF))
            return carry

        lax.fori_loop(0, 4, step, 0)

    def head():
        inv = s["rinv", LAYERS][...]
        dot_q = jnp.sum(s["q"][...] + s["q_in"][...], axis=1, keepdims=True)
        n_q = dot_q * inv
        seg_row = lax.broadcasted_iota(jnp.int32, (16, TOK), 0).astype(F32)
        onehots, rewards, counts = [], [], []
        for core in range(2):
            onehot = (s["packs"][core, 2:3, :] == seg_row).astype(F32)
            count = jnp.sum(onehot, axis=1, keepdims=True)
            total = jnp.dot(
                onehot,
                n_q[core * TOK : (core + 1) * TOK],
                precision=lax.Precision.HIGHEST,
                preferred_element_type=F32,
            )
            onehots.append(onehot)
            counts.append(count)
            rewards.append(total / count)
        place = lax.broadcasted_iota(jnp.int32, (8, 128), 0)
        lane = lax.broadcasted_iota(jnp.int32, (8, 128), 1)
        real = lane < 8
        for core in range(2):
            d_reward = []
            for k in range(2):
                order = s["packs"][core, 3 + k : 4 + k, 0:128]
                chosen = jnp.where(real & (order == place.astype(F32)), 1.0, 0.0)
                reward = rewards[core][8 * k : 8 * k + 8]
                placed = jnp.sum(chosen * reward, axis=0, keepdims=True)
                expo = jnp.exp(placed)
                suffix = jnp.sum(
                    jnp.where(real & (lane >= place), expo, 0.0), axis=1, keepdims=True
                )
                prefix = jnp.sum(
                    jnp.where(place <= lane, 1.0 / suffix, 0.0), axis=0, keepdims=True
                )
                d_placed = -1.0 + expo * prefix
                d_reward.append(
                    jnp.sum(jnp.where(chosen > 0.0, d_placed, 0.0), axis=1, keepdims=True)
                )
            scaled = jnp.concatenate(d_reward, axis=0) / counts[core]
            coef = lax.dot_general(
                onehots[core],
                jnp.broadcast_to(scaled, (16, 128)),
                (((0,), (0,)), ((), ())),
                precision=lax.Precision.HIGHEST,
                preferred_element_type=F32,
            )
            rows = pl.ds(core * TOK, TOK)
            inv_c = inv[core * TOK : (core + 1) * TOK]
            first = coef * inv_c
            s["coef"][rows, :] = first
            s["tok"][rows, :] = (
                first * inv_c * inv_c * dot_q[core * TOK : (core + 1) * TOK] * (1.0 / WIDTH)
            )
        vec = s["coef"][...].T[:8]
        hi = vec.astype(BF16)
        lo = (vec - hi.astype(F32)).astype(BF16)
        s["vec"][...] = jnp.concatenate([hi.astype(F32), lo.astype(F32)], axis=0).astype(BF16)

    def top(j):
        h, g = s["h", LAYERS], s["gb", LAYERS - 1]
        row = lax.broadcasted_iota(jnp.int32, (EXTRA, 256), 0)
        for i in range(4):
            vec = jnp.dot(s["vec"][...], h[i, j], preferred_element_type=F32)
            vec = jnp.where(row == 0, vec[0:1] + vec[8:9], 0.0).astype(BF16)
            g[0, i, j, pl.ds(R, EXTRA)] = vec[:, :HALF]
            g[1, i, j, pl.ds(R, EXTRA)] = vec[:, HALF:]
            hg = s["hg"][i, j, 0:1, :]
            for r in range(0, ROWS, CHUNK):
                rows = pl.ds(r, CHUNK)
                v = h[i, j, rows, :].astype(F32)
                v = lanes2(s["coef"][rows, :]) * hg - v * lanes2(s["tok"][rows, :])
                h[i, j, rows, :] = v.astype(BF16)

    def back_up(l):
        g, out = s["h", LAYERS], s["da", l]
        out[...] = jnp.zeros_like(out)

        def step(i, carry):
            lhs = jnp.concatenate([g[i, j] for j in range(4)], axis=1)
            rhs = jnp.concatenate([weights_out(l, i, j) for j in range(4)], axis=1)
            out[...] += lax.dot_general(lhs, rhs, NT, preferred_element_type=F32)
            return carry

        lax.fori_loop(0, 4, step, 0)

    def partial(lhs, wide, out, blocks):
        for i, j in blocks:
            v = jnp.dot(lhs[...], wide[i, j], preferred_element_type=F32).astype(BF16)
            out[0, i, j, pl.ds(0, R)] = v[:, :HALF]
            out[1, i, j, pl.ds(0, R)] = v[:, HALF:]

    def inner(l):
        v = s["z_in", l][...]
        inv = s["rinv", l][...]
        sigm = jax.nn.sigmoid(v)
        dz = (s["da", l][...] + s["da_in", l][...]) * sigm * (1.0 + v * (1.0 - sigm))
        mean = jnp.sum(dz * v, axis=1, keepdims=True) * (1.0 / WIDTH)
        s["tok"][...] = inv * inv * mean
        dz = dz * inv
        s["dzr"][...] = dz.astype(BF16)
        s["dzr_t"][...] = dz.T.astype(BF16)

    def back_down(l):
        g, h, w = s["h", LAYERS], s["h", l], s["wa", l]

        def step(i, carry):
            for j in range(4):
                rhs = w[i, j].reshape(2 * HALF, R)
                for r in range(0, ROWS, CHUNK):
                    rows = pl.ds(r, CHUNK)
                    du = lax.dot_general(s["dzr"][rows, :], rhs, NT, preferred_element_type=F32)
                    v = h[i, j, rows, :].astype(F32) * lanes2(s["tok"][rows, :])
                    g[i, j, rows, :] = (g[i, j, rows, :].astype(F32) + (du - v)).astype(BF16)
            return carry

        lax.fori_loop(0, 4, step, 0)

    in0, in1, in2 = (gather_in(l) for l in range(LAYERS))
    out0, out1, out2 = (gather_out(l) for l in range(LAYERS))
    core_send, core_recv = s["send"].at[N_SEMS - 1], s["recv"].at[N_SEMS - 1]
    def core_copy(src, dst):
        return pltpu.make_async_remote_copy(
            src_ref=src,
            dst_ref=dst,
            send_sem=core_send,
            recv_sem=core_recv,
            device_id=to_core,
            device_id_type=MESH,
        )
    go(in0)
    go(out0)
    def swap_hidden(i, carry):
        yy, zz = i // 4, i % 4
        for xx in range(2):
            col = pl.multiple_of(yy * 2048 + xx * 1024 + zz * 256 + other * HALF, HALF)
            core_copy(
                hidden.at[:, pl.ds(col, HALF)],
                s["h", 0].at[yy * c + zz * other, zz * c + yy * other, my_rows, pl.ds(xx * HALF, HALF)],
            ).start()
        return carry
    lax.fori_loop(0, 16, swap_hidden, 0)
    go(in1)
    go(out1)
    for copy in local_small:
        copy.wait()
    go(in2)
    go(out2)
    s["packs"][c, 2:3, :] = s["seg"][...].astype(F32)
    s["packs"][c, 3:5, 0:8] = s["ranks"][0].astype(F32)
    packs = send(s["packs"].at[c], s["packs"].at[c], to_core)
    go(in0)
    go(out0)
    go(in1)
    go(out1)
    go(in2)
    go(out2)
    block = s["h", 0].at[:, :, my_rows]
    pltpu.make_async_copy(block, block, hidden_sem).wait()
    swapped = core_copy(block, s["h", 0].at[:, :, their_rows])
    swapped.wait_recv()
    swapped.wait_send()
    squares(0)
    sq = send(s["sq", 0], s["sq_in", 0], to_core)
    go(in0)
    go(out0)
    go(in1)
    go(out1)
    arrived(sq)
    inverse(0)
    go(out0)
    go(in0)
    down(0)
    zc = send(s["z", 0], s["z_in", 0], to_core)
    go(out1)
    go(in2)
    go(out2)
    arrived(zc)
    activate(0)
    go(out0)
    up(0)
    sq = send(s["sq", 1], s["sq_in", 1], to_core)
    go(in1)
    go(out2)
    down(1)
    zc = send(s["z", 1], s["z_in", 1], to_core)
    arrived(sq)
    inverse(1)
    arrived(zc)
    activate(1)
    go(out1)
    up(1)
    sq = send(s["sq", 2], s["sq_in", 2], to_core)
    go(in2)
    down(2)
    zc = send(s["z", 2], s["z_in", 2], to_core)
    go(out2)
    gains()
    arrived(sq)
    inverse(2)
    arrived(zc)
    activate(2)
    up(2)
    sq = send(s["sq", 3], s["sq_in", 3], to_core)
    qc = send(s["q"], s["q_in"], to_core)
    arrived(packs, sq)
    inverse(3)
    arrived(qc)
    head()
    out2 = scatter_out(2)
    go(out2)
    back_up(2)
    dc = send(s["da", 2], s["da_in", 2], to_core)
    arrived(dc)
    inner(2)
    in2 = scatter_in(2)
    go(in2)
    back_down(2)
    go(out2)
    back_up(1)
    dc = send(s["da", 1], s["da_in", 1], to_core)
    out1 = scatter_out(1)
    go(out1)
    go(in2)
    go(out2)
    arrived(dc)
    inner(1)
    in1 = scatter_in(1)
    go(in1)
    go(out1)
    back_down(1)
    go(in2)
    go(out2)
    back_up(0)
    dc = send(s["da", 0], s["da_in", 0], to_core)
    out0 = scatter_out(0)
    go(out0)
    go(in1)
    go(out1)
    arrived(dc)
    inner(0)
    in0 = scatter_in(0)
    go(in0)
    go(out0)
    go(out2)
    go(in1)
    go(out1)
    go(in0)
    go(out0)
    go(in2)
    go(out2)
    go(in1)
    go(in2)
    go(out1)
    go(out2)
    go(in0)
    go(out0)
    go(in1)
    go(in2)
    go(out1)
    go(in0)
    go(out0)
    go(in1)
    go(out1)
    go(in0)
    go(out0)
    go(in0)
    go(out0)
    for copy in started:
        copy.wait_send()
    for copy in leaving:
        copy.wait()

def deliver(*refs):
    for i in range(4):
        refs[i + 4][...] = refs[i][...]

def body(hidden, seg_ids, ranks, adapter_in, adapter_out, score_head, final_gain):
    vmem = pl.BlockSpec(memory_space=pltpu.VMEM)
    hbm = pl.BlockSpec(memory_space=pl.ANY)
    shapes = (
        jax.ShapeDtypeStruct((LAYERS, 2 * HALF, R), F32),
        jax.ShapeDtypeStruct((LAYERS, R, 2 * HALF), F32),
        jax.ShapeDtypeStruct((2 * HALF,), F32),
        jax.ShapeDtypeStruct((2 * HALF,), F32),
    )
    grads = pl.pallas_call(
        kernel,
        out_shape=shapes,
        in_specs=[hbm] * 7,
        out_specs=(hbm,) * 4,
        scratch_shapes=list(scratch().values()),
        compiler_params=pltpu.CompilerParams(
            collective_id=0, has_side_effects=True, vmem_limit_bytes=60 * 1024 * 1024
        ),
        name="adapters",
    )(hidden, seg_ids, ranks, adapter_in, adapter_out, score_head, final_gain)
    return pl.pallas_call(
        deliver,
        out_shape=shapes,
        in_specs=[vmem] * 4,
        out_specs=(vmem,) * 4,
        name="deliver",
    )(*grads)

def solution(mesh):
    placed = (
        P(("rep", "shard"), None),
        P(("rep", "shard"), None),
        P(("rep", "shard"), None, None),
        P(None, "shard", None),
        P(None, None, "shard"),
        P("shard"),
        P("shard"),
    )
    return jax.shard_map(
        body,
        mesh=mesh,
        in_specs=placed,
        out_specs=(P(None, "shard", None), P(None, None, "shard"), P("shard"), P("shard")),
        check_vma=False,
    )
```

```python
import jax
import jax.numpy as jnp
from jax import lax
from jax.experimental import pallas as pl
from jax.experimental.pallas import tpu as pltpu
from jax.sharding import PartitionSpec as P

EPS = 1e-06
MESH = pl.DeviceIdType.MESH
F32 = jnp.float32
BF16 = jnp.bfloat16
LAYERS = 3
WIDTH = 8192
TOK = 256
ROWS = 2 * TOK
R = 128
HALF = 128
EXTRA = 16
N_SEMS = 240
NT = (((1,), (1,)), ((), ()))
CHUNK = 256

def unit_rows(layer):
    return R + EXTRA if layer == LAYERS - 1 else R

def scratch():
    shapes = {}
    for level in range(LAYERS + 1):
        shapes["h", level] = pltpu.VMEM((4, 4, ROWS, 2 * HALF), BF16)
        shapes["sq", level] = pltpu.VMEM((ROWS, 128), F32)
        shapes["sq_in", level] = pltpu.VMEM((ROWS, 128), F32)
        shapes["rinv", level] = pltpu.VMEM((ROWS, 128), F32)
    for layer in range(LAYERS):
        rows = unit_rows(layer)
        shapes["own", layer] = pltpu.VMEM((rows, HALF), BF16)
        shapes["wa", layer] = pltpu.VMEM((4, 4, 2, HALF, R), BF16)
        shapes["wb", layer] = pltpu.VMEM((2, 4, 4, rows, HALF), BF16)
        shapes["z", layer] = pltpu.VMEM((ROWS, R), F32)
        shapes["z_in", layer] = pltpu.VMEM((ROWS, R), F32)
        shapes["act_t", layer] = pltpu.VMEM((R, ROWS), BF16)
        shapes["da", layer] = pltpu.VMEM((ROWS, R), F32)
        shapes["da_in", layer] = pltpu.VMEM((ROWS, R), F32)
        shapes["ga", layer] = pltpu.VMEM((2, 4, 4, R, HALF), BF16)
        shapes["ga1", layer] = pltpu.VMEM((2, 4, R, HALF), BF16)
        shapes["ga2", layer] = pltpu.VMEM((2, 2, 4, R, HALF), BF16)
        shapes["ga3", layer] = pltpu.VMEM((2, 4, R, HALF), BF16)
        shapes["ga4", layer] = pltpu.VMEM((2, R, HALF), BF16)
        shapes["ga5", layer] = pltpu.VMEM((2, R, HALF), F32)
        shapes["ga6", layer] = pltpu.VMEM((2, R, HALF), BF16)
        shapes["gb", layer] = pltpu.VMEM((2, 4, 4, rows, HALF), BF16)
        shapes["gb1", layer] = pltpu.VMEM((4, 4, rows, HALF), BF16)
        shapes["gb2", layer] = pltpu.VMEM((4, rows, HALF), BF16)
        shapes["gb3", layer] = pltpu.VMEM((2, 4, rows, HALF), BF16)
        shapes["gb4", layer] = pltpu.VMEM((3, rows, HALF), BF16)
        shapes["gb5", layer] = pltpu.VMEM((2, rows, HALF), BF16)
        shapes["gb6", layer] = pltpu.VMEM((2, rows, HALF), F32)
        shapes["gb7", layer] = pltpu.VMEM((2, rows, HALF), BF16)
    shapes["act"] = pltpu.VMEM((ROWS, R), BF16)
    shapes["dzr"] = pltpu.VMEM((ROWS, R), BF16)
    shapes["dzr_t"] = pltpu.VMEM((R, ROWS), BF16)
    shapes["tok"] = pltpu.VMEM((ROWS, 128), F32)
    shapes["q"] = pltpu.VMEM((ROWS, 128), F32)
    shapes["q_in"] = pltpu.VMEM((ROWS, 128), F32)
    shapes["coef"] = pltpu.VMEM((ROWS, 128), F32)
    shapes["vec"] = pltpu.VMEM((16, ROWS), BF16)
    shapes["hg"] = pltpu.VMEM((4, 4, 8, 2 * HALF), F32)
    shapes["seg"] = pltpu.VMEM((1, TOK), jnp.int32)
    shapes["ranks"] = pltpu.VMEM((1, 2, 8), jnp.int32)
    shapes["score"] = pltpu.VMEM((2 * HALF,), BF16)
    shapes["gain"] = pltpu.VMEM((2 * HALF,), BF16)
    shapes["out_in"] = pltpu.VMEM((LAYERS, 2 * HALF, R), F32)
    shapes["out_out"] = pltpu.VMEM((LAYERS, R, 2 * HALF), F32)
    shapes["out_head"] = pltpu.VMEM((2 * HALF,), F32)
    shapes["out_gain"] = pltpu.VMEM((2 * HALF,), F32)
    shapes["packs"] = pltpu.VMEM((2, 8, 256), F32)
    shapes["send"] = pltpu.SemaphoreType.DMA((N_SEMS,))
    shapes["recv"] = pltpu.SemaphoreType.DMA((N_SEMS,))
    shapes["local"] = pltpu.SemaphoreType.DMA((32,))
    return shapes

def kernel(
    hidden, seg_ids, ranks, w_in, w_out, score_head, final_gain,
    grad_in, grad_out, grad_head, grad_gain, *refs
):
    s = dict(zip(scratch(), refs))
    rep, shard = lax.axis_index("rep"), lax.axis_index("shard")
    xh, c = rep // 2, rep % 2
    y, xl, z = shard // 8, (shard // 4) % 2, shard % 4
    other = 1 - c
    low, high = pl.ds(0, 2), pl.ds(2, 2)
    p, q = y * other + z * c, z * other + y * c
    pp, p2, pm = (p + 1) % 4, (p + 2) % 4, (p + 3) % 4
    qp, q2, qm = (q + 1) % 4, (q + 2) % 4, (q + 3) % 4

    def device(x_by, p_by, q_by):
        x = (xh * 2 + xl + x_by) % 4
        y_to = (y + p_by * other + q_by * c) % 4
        z_to = (z + q_by * other + p_by * c) % 4
        return (x // 2 * 2 + c, y_to * 8 + x % 2 * 4 + z_to)

    to_p = [device(0, by, 0) for by in range(1, 4)]
    to_q = [device(0, 0, by) for by in range(1, 4)]
    to_xp = [device(1, 0, by) for by in range(4)]
    to_xm = [device(3, 0, by) for by in range(4)]
    to_core = (xh * 2 + other, shard)
    to_rep = ((1 - xh) * 2 + c, shard)
    to_both = ((1 - xh) * 2 + other, shard)
    to_x = to_xp[:2] + to_xm[2:]

    used = [0, 0]
    started = []

    def send(src, dst, to):
        i = used[0]
        used[0] += 1
        copy = pltpu.make_async_remote_copy(
            src_ref=src,
            dst_ref=dst,
            send_sem=s["send"].at[i],
            recv_sem=s["recv"].at[i],
            device_id=to,
            device_id_type=MESH,
        )
        copy.start()
        started.append(copy)
        return copy

    def local(src, dst):
        copy = pltpu.make_async_copy(src, dst, s["local"].at[used[1]])
        used[1] += 1
        copy.start()
        return copy

    def arrived(*copies):
        for copy in copies:
            copy.wait_recv()

    mine = pl.ds(pl.multiple_of(c * HALF, HALF), HALF)
    my_rows = pl.ds(pl.multiple_of(c * TOK, TOK), TOK)
    their_rows = pl.ds(pl.multiple_of(other * TOK, TOK), TOK)
    def head_row():
        return s["score"][...].astype(F32).reshape(1, 2 * HALF)

    def gain_row():
        return s["gain"][...].astype(F32).reshape(1, 2 * HALF)

    barrier = pltpu.get_barrier_semaphore()
    partners = (*to_p, *to_q, *to_xp, *to_xm, to_core, to_rep, to_both)
    for partner in partners:
        pl.semaphore_signal(barrier, inc=1, device_id=partner, device_id_type=MESH)

    local_in = [
        local(w_in.at[l, mine], s["wa", l].at[p, q, xl]) for l in range(LAYERS)
    ]
    local_out = [
        local(w_out.at[l, :, mine], s["own", l].at[pl.ds(0, R)]) for l in range(LAYERS)
    ]
    local_small = [
        local(src, s[name])
        for src, name in (
            (seg_ids, "seg"),
            (ranks, "ranks"),
            (score_head, "score"),
            (final_gain, "gain"),
        )
    ]

    hidden_sem = s["local"].at[31]

    def load_hidden(i, carry):
        yy, zz = i // 4, i % 4
        for xx in range(2):
            col = pl.multiple_of(yy * 2048 + xx * 1024 + zz * 256 + c * HALF, HALF)
            pltpu.make_async_copy(
                hidden.at[:, pl.ds(col, HALF)],
                s["h", 0].at[yy * other + zz * c, zz * other + yy * c, my_rows, pl.ds(xx * HALF, HALF)],
                hidden_sem,
            ).start()
        return carry

    lax.fori_loop(0, 16, load_hidden, 0)
    pl.semaphore_wait(barrier, len(partners))

    def gather_in(l):
        w, src = s["wa", l], w_in.at[l, mine]
        copies = [send(src, w.at[p, q, xl], to) for to in (to_q if l else (*to_q, *to_x))]
        yield
        local_in[l].wait()
        arrived(*copies)
        if l:
            copies = [
                send(w.at[p, low, xl], w.at[p, low, xl], to_xp[0]),
                send(w.at[p, high, xl], w.at[p, high, xl], to_xm[0]),
            ]
            yield
            arrived(*copies)
        a = send(w.at[p, low], w.at[p, low], to_p[0])
        b = send(w.at[p, high], w.at[p, high], to_p[2])
        copies = [
            send(w.at[p, high], w.at[p, high], to_p[0]),
            send(w.at[p, low], w.at[p, low], to_p[2]),
        ]
        yield
        arrived(a, b)
        copies += [
            send(w.at[pm, low], w.at[pm, low], to_p[0]),
            send(w.at[pp, high], w.at[pp, high], to_p[2]),
        ]
        yield
        arrived(*copies)
        yield

    def gather_out(l):
        w, own, rows = s["wb", l], s["own", l], unit_rows(l)
        local_out[l].wait()
        if rows > R:
            both = head_row() * gain_row()
            both = both[:, :HALF] * (1 - c).astype(F32) + both[:, HALF:] * c.astype(F32)
            hi = both.astype(BF16)
            lo = (both - hi.astype(F32)).astype(BF16)
            row = lax.broadcasted_iota(jnp.int32, (EXTRA, HALF), 0)
            own[pl.ds(R, EXTRA), :] = jnp.where(
                row == 0, hi.astype(F32), jnp.where(row == 1, lo.astype(F32), 0.0)
            ).astype(BF16)
        copies = [send(own, w.at[xl, p, q], to) for to in to_p]
        kept = local(own, w.at[xl, p, q])
        yield
        kept.wait()
        arrived(*copies)
        a = send(w.at[xl, low, q], w.at[xl, low, q], to_q[0])
        b = send(w.at[xl, high, q], w.at[xl, high, q], to_q[2])
        copies = [
            send(w.at[xl, high, q], w.at[xl, high, q], to_q[0]),
            send(w.at[xl, low, q], w.at[xl, low, q], to_q[2]),
        ]
        across = [
            send(w.at[xl, low, q], w.at[xl, low, q], to_xp[0]),
            send(w.at[xl, high, q], w.at[xl, high, q], to_xm[0]),
        ]
        yield
        arrived(a, b)
        copies += [
            send(w.at[xl, low, qm], w.at[xl, low, qm], to_q[0]),
            send(w.at[xl, high, qp], w.at[xl, high, qp], to_q[2]),
        ]
        across += [
            send(w.at[xl, low, qm], w.at[xl, low, qm], to_xp[0]),
            send(w.at[xl, high, qp], w.at[xl, high, qp], to_xm[0]),
        ]
        yield
        arrived(*copies)
        across += [
            send(w.at[xl, low, qp], w.at[xl, low, qp], to_xp[0]),
            send(w.at[xl, high, qm], w.at[xl, high, qm], to_xm[0]),
            send(w.at[xl, low, q2], w.at[xl, low, q2], to_xp[0]),
            send(w.at[xl, high, q2], w.at[xl, high, q2], to_xm[0]),
        ]
        yield
        arrived(*across)
        yield

    def total(*parts):
        value = parts[0].astype(F32)
        for part in parts[1:]:
            value = value + part.astype(F32)
        return value

    def finish(own, whole, far, l, store):
        copies = [send(own.at[xh], own.at[xh], to_rep)]
        if l == 0:
            copies += [send(own.at[xh], far.at[xh], to) for to in (to_core, to_both)]
        yield
        arrived(*copies)
        whole[c] = total(own[0], own[1])
        if l == 0:
            whole[other] = total(far[0], far[1])
        else:
            copy = send(whole.at[c], whole.at[c], to_core)
            yield
            arrived(copy)
        for half in range(2):
            store(l, half, whole[half])
        yield

    def scatter_out(l):
        g = s["gb", l]
        r1, r2, r3, r4, r5, r6, r7 = (s["gb%d" % i, l] for i in range(1, 8))
        across = []
        for j in (q2, qp, qm, q):
            if l == LAYERS - 1:
                top(j)
            partial(s["act_t", l], s["h", LAYERS], g, [(i, j) for i in range(4)])
            across += [
                send(g.at[1 - xl, low, j], r1.at[low, j], to_xp[0]),
                send(g.at[1 - xl, high, j], r1.at[high, j], to_xm[0]),
            ]
        yield
        arrived(*across[:2])
        for i in range(4):
            g[xl, i, q2] = total(g[xl, i, q2], r1[i, q2]).astype(BF16)
        a = send(g.at[xl, low, q2], r2.at[low], to_q[0])
        b = send(g.at[xl, high, q2], r2.at[high], to_q[2])
        yield
        arrived(*across[2:6])
        for i in range(2):
            g[xl, i + 2, qp] = total(g[xl, i + 2, qp], r1[i + 2, qp]).astype(BF16)
            g[xl, i, qm] = total(g[xl, i, qm], r1[i, qm]).astype(BF16)
        copies = [
            send(g.at[xl, high, qp], r3.at[0, high], to_q[0]),
            send(g.at[xl, low, qm], r3.at[1, low], to_q[2]),
        ]
        arrived(a, b)
        for i in range(2):
            g[xl, i, qp] = total(g[xl, i, qp], r1[i, qp], r2[i]).astype(BF16)
            g[xl, i + 2, qm] = total(g[xl, i + 2, qm], r1[i + 2, qm], r2[i + 2]).astype(BF16)
        copies += [
            send(g.at[xl, low, qp], r3.at[0, low], to_q[0]),
            send(g.at[xl, high, qm], r3.at[1, high], to_q[2]),
        ]
        yield
        arrived(*across[6:], *copies)
        for i in range(4):
            g[xl, i, q] = total(g[xl, i, q], r1[i, q], r3[0, i], r3[1, i]).astype(BF16)
        copies = [send(g.at[xl, (p + 1 + k) % 4, q], r4.at[k], to_p[k]) for k in range(3)]
        yield
        arrived(*copies)
        r5[xh] = total(g[xl, p, q], r4[0], r4[1], r4[2]).astype(BF16)
        yield from finish(r5, r6, r7, l, store_out)

    def scatter_in(l):
        g = s["ga", l]
        r1, r2, r3, r4, r5, r6 = (s["ga%d" % i, l] for i in range(1, 7))
        partial(s["dzr_t"], s["h", l], g, [(p2, j) for j in range(4)])
        a = send(g.at[:, p2, low], r1.at[:, low], to_p[0])
        b = send(g.at[:, p2, high], r1.at[:, high], to_p[2])
        partial(s["dzr_t"], s["h", l], g, [(pp, j) for j in (2, 3)] + [(pm, j) for j in (0, 1)])
        copies = [
            send(g.at[:, pp, high], r2.at[0, :, high], to_p[0]),
            send(g.at[:, pm, low], r2.at[1, :, low], to_p[2]),
        ]
        partial(s["dzr_t"], s["h", l], g, [(pp, j) for j in (0, 1)] + [(pm, j) for j in (2, 3)])
        partial(s["dzr_t"], s["h", l], g, [(p, j) for j in range(4)])
        yield
        arrived(a, b)
        for x in range(2):
            for j in range(2):
                g[x, pp, j] = total(g[x, pp, j], r1[x, j]).astype(BF16)
                g[x, pm, j + 2] = total(g[x, pm, j + 2], r1[x, j + 2]).astype(BF16)
        copies += [
            send(g.at[:, pp, low], r2.at[0, :, low], to_p[0]),
            send(g.at[:, pm, high], r2.at[1, :, high], to_p[2]),
        ]
        yield
        arrived(*copies)
        for x in range(2):
            for j in range(4):
                g[x, p, j] = total(g[x, p, j], r2[0, x, j], r2[1, x, j]).astype(BF16)
        copies = [send(g.at[xl, p, (q + 1 + k) % 4], r3.at[0, k + 1], to_q[k]) for k in range(3)]
        copies += [send(g.at[1 - xl, p, (q + k) % 4], r3.at[1, k], to_x[k]) for k in range(4)]
        yield
        arrived(*copies)
        r4[xh] = total(
            g[xl, p, q], *[r3[0, k] for k in range(1, 4)], *[r3[1, k] for k in range(4)]
        ).astype(BF16)
        yield from finish(r4, r5, r6, l, store_in)

    vecs, leaving = [], []

    def store_in(l, half, total):
        s["out_in"][l, pl.ds(half * HALF, HALF), :] = total.T
        if half == 1:
            leaving.append(local(s["out_in"].at[l], grad_in.at[l]))

    def store_out(l, half, total):
        lanes = pl.ds(half * HALF, HALF)
        s["out_out"][l, :, lanes] = total[:R]
        if half == 1:
            leaving.append(local(s["out_out"].at[l], grad_out.at[l]))
        if unit_rows(l) > R:
            vec = total[R : R + 8]
            row = lax.broadcasted_iota(jnp.int32, (8, HALF), 0)
            vec = jnp.sum(jnp.where(row == 0, vec, 0.0), axis=0, keepdims=True)
            vecs.append(vec)
            if half == 1:
                vec = jnp.concatenate(vecs, axis=1)
                s["out_head"][...] = (vec * gain_row()).reshape(2 * HALF)
                s["out_gain"][...] = (vec * head_row()).reshape(2 * HALF)
                leaving.append(local(s["out_head"], grad_head))
                leaving.append(local(s["out_gain"], grad_gain))

    def go(*jobs):
        for job in jobs:
            next(job, None)

    def lanes2(values):
        return jnp.concatenate([values, values], axis=1)

    def weights_out(l, i, j):
        w = s["wb", l]
        return jnp.concatenate([w[0, i, j, pl.ds(0, R)], w[1, i, j, pl.ds(0, R)]], axis=1)

    def squares(level):
        h, out = s["h", level], s["sq", level]
        out[...] = jnp.zeros_like(out)

        def step(i, carry):
            for r in range(0, ROWS, CHUNK):
                rows = pl.ds(r, CHUNK)
                total = out[rows, :]
                for j in range(4):
                    v = h[i, j, rows, :].astype(F32)
                    v = v * v
                    total = total + (v[:, :128] + v[:, 128:])
                out[rows, :] = total
            return carry

        lax.fori_loop(0, 4, step, 0)

    def down(l):
        h, w, out = s["h", l], s["wa", l], s["z", l]
        out[...] = jnp.zeros_like(out)

        def step(i, carry):
            lhs = jnp.concatenate([h[i, j] for j in range(4)], axis=1)
            out[...] += jnp.dot(lhs, w[i].reshape(4 * 2 * HALF, R), preferred_element_type=F32)
            return carry

        lax.fori_loop(0, 4, step, 0)

    def inverse(level):
        total = jnp.sum(s["sq", level][...] + s["sq_in", level][...], axis=1, keepdims=True)
        inv = lax.rsqrt(total * (1.0 / WIDTH) + EPS)
        s["rinv", level][...] = jnp.broadcast_to(inv, (ROWS, 128))

    def activate(l):
        v = (s["z", l][...] + s["z_in", l][...]) * s["rinv", l][...]
        s["z_in", l][...] = v
        active = v * jax.nn.sigmoid(v)
        s["act"][...] = active.astype(BF16)
        s["act_t", l][...] = active.T.astype(BF16)

    def up(l):
        h, out, sq = s["h", l], s["h", l + 1], s["sq", l + 1]
        last = l == LAYERS - 1
        sq[...] = jnp.zeros_like(sq)
        if last:
            s["q"][...] = jnp.zeros_like(s["q"])

        def step(i, carry):
            for j in range(4):
                w = weights_out(l, i, j)
                if last:
                    hg = s["hg"][i, j, 0:1, :]
                for r in range(0, ROWS, CHUNK):
                    rows = pl.ds(r, CHUNK)
                    v = jnp.dot(s["act"][rows, :], w, preferred_element_type=F32)
                    v = (h[i, j, rows, :].astype(F32) + v).astype(BF16)
                    out[i, j, rows, :] = v
                    v = v.astype(F32)
                    if last:
                        t = v * hg
                        s["q"][rows, :] += t[:, :128] + t[:, 128:]
                    v = v * v
                    sq[rows, :] += v[:, :128] + v[:, 128:]
            return carry

        lax.fori_loop(0, 4, step, 0)

    def gains():
        w = s["wb", LAYERS - 1]

        def step(i, carry):
            for j in range(4):
                for x in range(2):
                    rows = w[x, i, j, pl.ds(R, EXTRA)].astype(F32)
                    both = jnp.sum(rows, axis=0, keepdims=True)
                    s["hg"][i, j, :, pl.ds(x * HALF, HALF)] = jnp.broadcast_to(both, (8, HALF))
            return carry

        lax.fori_loop(0, 4, step, 0)

    def head():
        inv = s["rinv", LAYERS][...]
        dot_q = jnp.sum(s["q"][...] + s["q_in"][...], axis=1, keepdims=True)
        n_q = dot_q * inv
        seg_row = lax.broadcasted_iota(jnp.int32, (16, TOK), 0).astype(F32)
        onehots, rewards, counts = [], [], []
        for core in range(2):
            onehot = (s["packs"][core, 2:3, :] == seg_row).astype(F32)
            count = jnp.sum(onehot, axis=1, keepdims=True)
            total = jnp.dot(
                onehot,
                n_q[core * TOK : (core + 1) * TOK],
                precision=lax.Precision.HIGHEST,
                preferred_element_type=F32,
            )
            onehots.append(onehot)
            counts.append(count)
            rewards.append(total / count)
        place = lax.broadcasted_iota(jnp.int32, (8, 128), 0)
        lane = lax.broadcasted_iota(jnp.int32, (8, 128), 1)
        real = lane < 8
        for core in range(2):
            d_reward = []
            for k in range(2):
                order = s["packs"][core, 3 + k : 4 + k, 0:128]
                chosen = jnp.where(real & (order == place.astype(F32)), 1.0, 0.0)
                reward = rewards[core][8 * k : 8 * k + 8]
                placed = jnp.sum(chosen * reward, axis=0, keepdims=True)
                expo = jnp.exp(placed)
                suffix = jnp.sum(
                    jnp.where(real & (lane >= place), expo, 0.0), axis=1, keepdims=True
                )
                prefix = jnp.sum(
                    jnp.where(place <= lane, 1.0 / suffix, 0.0), axis=0, keepdims=True
                )
                d_placed = -1.0 + expo * prefix
                d_reward.append(
                    jnp.sum(jnp.where(chosen > 0.0, d_placed, 0.0), axis=1, keepdims=True)
                )
            scaled = jnp.concatenate(d_reward, axis=0) / counts[core]
            coef = lax.dot_general(
                onehots[core],
                jnp.broadcast_to(scaled, (16, 128)),
                (((0,), (0,)), ((), ())),
                precision=lax.Precision.HIGHEST,
                preferred_element_type=F32,
            )
            rows = pl.ds(core * TOK, TOK)
            inv_c = inv[core * TOK : (core + 1) * TOK]
            first = coef * inv_c
            s["coef"][rows, :] = first
            s["tok"][rows, :] = (
                first * inv_c * inv_c * dot_q[core * TOK : (core + 1) * TOK] * (1.0 / WIDTH)
            )
        vec = s["coef"][...].T[:8]
        hi = vec.astype(BF16)
        lo = (vec - hi.astype(F32)).astype(BF16)
        s["vec"][...] = jnp.concatenate([hi.astype(F32), lo.astype(F32)], axis=0).astype(BF16)

    def top(j):
        h, g = s["h", LAYERS], s["gb", LAYERS - 1]
        row = lax.broadcasted_iota(jnp.int32, (EXTRA, 256), 0)
        for i in range(4):
            vec = jnp.dot(s["vec"][...], h[i, j], preferred_element_type=F32)
            vec = jnp.where(row == 0, vec[0:1] + vec[8:9], 0.0).astype(BF16)
            g[0, i, j, pl.ds(R, EXTRA)] = vec[:, :HALF]
            g[1, i, j, pl.ds(R, EXTRA)] = vec[:, HALF:]
            hg = s["hg"][i, j, 0:1, :]
            for r in range(0, ROWS, CHUNK):
                rows = pl.ds(r, CHUNK)
                v = h[i, j, rows, :].astype(F32)
                v = lanes2(s["coef"][rows, :]) * hg - v * lanes2(s["tok"][rows, :])
                h[i, j, rows, :] = v.astype(BF16)

    def back_up(l):
        g, out = s["h", LAYERS], s["da", l]
        out[...] = jnp.zeros_like(out)

        def step(i, carry):
            lhs = jnp.concatenate([g[i, j] for j in range(4)], axis=1)
            rhs = jnp.concatenate([weights_out(l, i, j) for j in range(4)], axis=1)
            out[...] += lax.dot_general(lhs, rhs, NT, preferred_element_type=F32)
            return carry

        lax.fori_loop(0, 4, step, 0)

    def partial(lhs, wide, out, blocks):
        for i, j in blocks:
            v = jnp.dot(lhs[...], wide[i, j], preferred_element_type=F32).astype(BF16)
            out[0, i, j, pl.ds(0, R)] = v[:, :HALF]
            out[1, i, j, pl.ds(0, R)] = v[:, HALF:]

    def inner(l):
        v = s["z_in", l][...]
        inv = s["rinv", l][...]
        sigm = jax.nn.sigmoid(v)
        dz = (s["da", l][...] + s["da_in", l][...]) * sigm * (1.0 + v * (1.0 - sigm))
        mean = jnp.sum(dz * v, axis=1, keepdims=True) * (1.0 / WIDTH)
        s["tok"][...] = inv * inv * mean
        dz = dz * inv
        s["dzr"][...] = dz.astype(BF16)
        s["dzr_t"][...] = dz.T.astype(BF16)

    def back_down(l):
        g, h, w = s["h", LAYERS], s["h", l], s["wa", l]

        def step(i, carry):
            for j in range(4):
                rhs = w[i, j].reshape(2 * HALF, R)
                for r in range(0, ROWS, CHUNK):
                    rows = pl.ds(r, CHUNK)
                    du = lax.dot_general(s["dzr"][rows, :], rhs, NT, preferred_element_type=F32)
                    v = h[i, j, rows, :].astype(F32) * lanes2(s["tok"][rows, :])
                    g[i, j, rows, :] = (g[i, j, rows, :].astype(F32) + (du - v)).astype(BF16)
            return carry

        lax.fori_loop(0, 4, step, 0)

    in0, in1, in2 = (gather_in(l) for l in range(LAYERS))
    out0, out1, out2 = (gather_out(l) for l in range(LAYERS))
    core_send, core_recv = s["send"].at[N_SEMS - 1], s["recv"].at[N_SEMS - 1]
    def core_copy(src, dst):
        return pltpu.make_async_remote_copy(
            src_ref=src,
            dst_ref=dst,
            send_sem=core_send,
            recv_sem=core_recv,
            device_id=to_core,
            device_id_type=MESH,
        )
    go(in0)
    go(out0)
    def swap_hidden(i, carry):
        yy, zz = i // 4, i % 4
        for xx in range(2):
            col = pl.multiple_of(yy * 2048 + xx * 1024 + zz * 256 + other * HALF, HALF)
            core_copy(
                hidden.at[:, pl.ds(col, HALF)],
                s["h", 0].at[yy * c + zz * other, zz * c + yy * other, my_rows, pl.ds(xx * HALF, HALF)],
            ).start()
        return carry
    lax.fori_loop(0, 16, swap_hidden, 0)
    go(in1)
    go(out1)
    for copy in local_small:
        copy.wait()
    go(in2)
    go(out2)
    s["packs"][c, 2:3, :] = s["seg"][...].astype(F32)
    s["packs"][c, 3:5, 0:8] = s["ranks"][0].astype(F32)
    packs = send(s["packs"].at[c], s["packs"].at[c], to_core)
    go(in0)
    go(out0)
    go(in1)
    go(out1)
    go(in2)
    go(out2)
    go(in0)
    go(out0)
    go(in1)
    block = s["h", 0].at[:, :, my_rows]
    pltpu.make_async_copy(block, block, hidden_sem).wait()
    swapped = core_copy(block, s["h", 0].at[:, :, their_rows])
    swapped.wait_recv()
    swapped.wait_send()
    squares(0)
    sq = send(s["sq", 0], s["sq_in", 0], to_core)
    go(out1)
    go(in2)
    arrived(sq)
    inverse(0)
    go(out0)
    go(in0)
    down(0)
    zc = send(s["z", 0], s["z_in", 0], to_core)
    go(in1)
    go(out1)
    go(out2)
    arrived(zc)
    activate(0)
    go(out0)
    up(0)
    sq = send(s["sq", 1], s["sq_in", 1], to_core)
    go(in1)
    go(in2)
    go(out2)
    down(1)
    zc = send(s["z", 1], s["z_in", 1], to_core)
    arrived(sq)
    inverse(1)
    arrived(zc)
    activate(1)
    go(out1)
    up(1)
    sq = send(s["sq", 2], s["sq_in", 2], to_core)
    go(in2)
    down(2)
    zc = send(s["z", 2], s["z_in", 2], to_core)
    arrived(sq)
    inverse(2)
    arrived(zc)
    activate(2)
    go(out2)
    gains()
    up(2)
    sq = send(s["sq", 3], s["sq_in", 3], to_core)
    qc = send(s["q"], s["q_in"], to_core)
    arrived(packs, sq)
    inverse(3)
    arrived(qc)
    head()
    out2 = scatter_out(2)
    go(out2)
    back_up(2)
    dc = send(s["da", 2], s["da_in", 2], to_core)
    arrived(dc)
    inner(2)
    in2 = scatter_in(2)
    go(in2)
    back_down(2)
    go(out2)
    back_up(1)
    dc = send(s["da", 1], s["da_in", 1], to_core)
    out1 = scatter_out(1)
    go(out1)
    go(in2)
    go(out2)
    arrived(dc)
    inner(1)
    in1 = scatter_in(1)
    go(in1)
    go(out1)
    back_down(1)
    go(in2)
    go(out2)
    back_up(0)
    dc = send(s["da", 0], s["da_in", 0], to_core)
    out0 = scatter_out(0)
    go(out0)
    go(in1)
    go(out1)
    arrived(dc)
    inner(0)
    in0 = scatter_in(0)
    go(in0)
    go(out0)
    go(out2)
    go(in1)
    go(out1)
    go(in0)
    go(out0)
    go(in2)
    go(out2)
    go(in1)
    go(in2)
    go(out1)
    go(out2)
    go(in0)
    go(out0)
    go(in1)
    go(in2)
    go(out1)
    go(in0)
    go(out0)
    go(in1)
    go(out1)
    go(in0)
    go(out0)
    go(in0)
    go(out0)
    for copy in started:
        copy.wait_send()
    for copy in leaving:
        copy.wait()

def deliver(*refs):
    for i in range(4):
        refs[i + 4][...] = refs[i][...]

def body(hidden, seg_ids, ranks, adapter_in, adapter_out, score_head, final_gain):
    vmem = pl.BlockSpec(memory_space=pltpu.VMEM)
    hbm = pl.BlockSpec(memory_space=pl.ANY)
    shapes = (
        jax.ShapeDtypeStruct((LAYERS, 2 * HALF, R), F32),
        jax.ShapeDtypeStruct((LAYERS, R, 2 * HALF), F32),
        jax.ShapeDtypeStruct((2 * HALF,), F32),
        jax.ShapeDtypeStruct((2 * HALF,), F32),
    )
    grads = pl.pallas_call(
        kernel,
        out_shape=shapes,
        in_specs=[hbm] * 7,
        out_specs=(hbm,) * 4,
        scratch_shapes=list(scratch().values()),
        compiler_params=pltpu.CompilerParams(
            collective_id=0, has_side_effects=True, vmem_limit_bytes=60 * 1024 * 1024
        ),
        name="adapters",
    )(hidden, seg_ids, ranks, adapter_in, adapter_out, score_head, final_gain)
    return pl.pallas_call(
        deliver,
        out_shape=shapes,
        in_specs=[vmem] * 4,
        out_specs=(vmem,) * 4,
        name="deliver",
    )(*grads)

def solution(mesh):
    placed = (
        P(("rep", "shard"), None),
        P(("rep", "shard"), None),
        P(("rep", "shard"), None, None),
        P(None, "shard", None),
        P(None, None, "shard"),
        P("shard"),
        P("shard"),
    )
    return jax.shard_map(
        body,
        mesh=mesh,
        in_specs=placed,
        out_specs=(P(None, "shard", None), P(None, None, "shard"), P("shard"), P("shard")),
        check_vma=False,
    )
```

```python
import jax
import jax.numpy as jnp
from jax import lax
from jax.experimental import pallas as pl
from jax.experimental.pallas import tpu as pltpu
from jax.sharding import PartitionSpec as P

EPS = 1e-06
MESH = pl.DeviceIdType.MESH
F32 = jnp.float32
BF16 = jnp.bfloat16
LAYERS = 3
WIDTH = 8192
TOK = 256
ROWS = 2 * TOK
R = 128
HALF = 128
EXTRA = 16
N_SEMS = 240
NT = (((1,), (1,)), ((), ()))
CHUNK = 256

def unit_rows(layer):
    return R + EXTRA if layer == LAYERS - 1 else R

def scratch():
    shapes = {}
    for level in range(LAYERS + 1):
        shapes["h", level] = pltpu.VMEM((4, 4, ROWS, 2 * HALF), BF16)
        shapes["sq", level] = pltpu.VMEM((ROWS, 128), F32)
        shapes["sq_in", level] = pltpu.VMEM((ROWS, 128), F32)
        shapes["rinv", level] = pltpu.VMEM((ROWS, 128), F32)
    for layer in range(LAYERS):
        rows = unit_rows(layer)
        shapes["own", layer] = pltpu.VMEM((rows, HALF), BF16)
        shapes["wa", layer] = pltpu.VMEM((4, 4, 2, HALF, R), BF16)
        shapes["wb", layer] = pltpu.VMEM((2, 4, 4, rows, HALF), BF16)
        shapes["z", layer] = pltpu.VMEM((ROWS, R), F32)
        shapes["z_in", layer] = pltpu.VMEM((ROWS, R), F32)
        shapes["act_t", layer] = pltpu.VMEM((R, ROWS), BF16)
        shapes["da", layer] = pltpu.VMEM((ROWS, R), F32)
        shapes["da_in", layer] = pltpu.VMEM((ROWS, R), F32)
        shapes["ga", layer] = pltpu.VMEM((2, 4, 4, R, HALF), BF16)
        shapes["ga1", layer] = pltpu.VMEM((2, 4, R, HALF), BF16)
        shapes["ga2", layer] = pltpu.VMEM((2, 2, 4, R, HALF), BF16)
        shapes["ga3", layer] = pltpu.VMEM((2, 4, R, HALF), BF16)
        shapes["ga4", layer] = pltpu.VMEM((2, R, HALF), BF16)
        shapes["ga5", layer] = pltpu.VMEM((2, R, HALF), F32)
        shapes["ga6", layer] = pltpu.VMEM((2, R, HALF), BF16)
        shapes["gb", layer] = pltpu.VMEM((2, 4, 4, rows, HALF), BF16)
        shapes["gb1", layer] = pltpu.VMEM((4, 4, rows, HALF), BF16)
        shapes["gb2", layer] = pltpu.VMEM((4, rows, HALF), BF16)
        shapes["gb3", layer] = pltpu.VMEM((2, 4, rows, HALF), BF16)
        shapes["gb4", layer] = pltpu.VMEM((3, rows, HALF), BF16)
        shapes["gb5", layer] = pltpu.VMEM((2, rows, HALF), BF16)
        shapes["gb6", layer] = pltpu.VMEM((2, rows, HALF), F32)
        shapes["gb7", layer] = pltpu.VMEM((2, rows, HALF), BF16)
    shapes["act"] = pltpu.VMEM((ROWS, R), BF16)
    shapes["dzr"] = pltpu.VMEM((ROWS, R), BF16)
    shapes["dzr_t"] = pltpu.VMEM((R, ROWS), BF16)
    shapes["tok"] = pltpu.VMEM((ROWS, 128), F32)
    shapes["q"] = pltpu.VMEM((ROWS, 128), F32)
    shapes["q_in"] = pltpu.VMEM((ROWS, 128), F32)
    shapes["coef"] = pltpu.VMEM((ROWS, 128), F32)
    shapes["vec"] = pltpu.VMEM((16, ROWS), BF16)
    shapes["hg"] = pltpu.VMEM((4, 4, 8, 2 * HALF), F32)
    shapes["seg"] = pltpu.VMEM((1, TOK), jnp.int32)
    shapes["ranks"] = pltpu.VMEM((1, 2, 8), jnp.int32)
    shapes["score"] = pltpu.VMEM((2 * HALF,), BF16)
    shapes["gain"] = pltpu.VMEM((2 * HALF,), BF16)
    shapes["out_in"] = pltpu.VMEM((LAYERS, 2 * HALF, R), F32)
    shapes["out_out"] = pltpu.VMEM((LAYERS, R, 2 * HALF), F32)
    shapes["out_head"] = pltpu.VMEM((2 * HALF,), F32)
    shapes["out_gain"] = pltpu.VMEM((2 * HALF,), F32)
    shapes["packs"] = pltpu.VMEM((2, 8, 256), F32)
    shapes["send"] = pltpu.SemaphoreType.DMA((N_SEMS,))
    shapes["recv"] = pltpu.SemaphoreType.DMA((N_SEMS,))
    shapes["local"] = pltpu.SemaphoreType.DMA((32,))
    return shapes

def kernel(
    hidden, seg_ids, ranks, w_in, w_out, score_head, final_gain,
    grad_in, grad_out, grad_head, grad_gain, *refs
):
    s = dict(zip(scratch(), refs))
    rep, shard = lax.axis_index("rep"), lax.axis_index("shard")
    xh, c = rep // 2, rep % 2
    y, xl, z = shard // 8, (shard // 4) % 2, shard % 4
    other = 1 - c
    low, high = pl.ds(0, 2), pl.ds(2, 2)
    p, q = y * other + z * c, z * other + y * c
    pp, p2, pm = (p + 1) % 4, (p + 2) % 4, (p + 3) % 4
    qp, q2, qm = (q + 1) % 4, (q + 2) % 4, (q + 3) % 4

    def device(x_by, p_by, q_by):
        x = (xh * 2 + xl + x_by) % 4
        y_to = (y + p_by * other + q_by * c) % 4
        z_to = (z + q_by * other + p_by * c) % 4
        return (x // 2 * 2 + c, y_to * 8 + x % 2 * 4 + z_to)

    to_p = [device(0, by, 0) for by in range(1, 4)]
    to_q = [device(0, 0, by) for by in range(1, 4)]
    to_xp = [device(1, 0, by) for by in range(4)]
    to_xm = [device(3, 0, by) for by in range(4)]
    to_core = (xh * 2 + other, shard)
    to_rep = ((1 - xh) * 2 + c, shard)
    to_both = ((1 - xh) * 2 + other, shard)
    to_x = to_xp[:2] + to_xm[2:]

    used = [0, 0]
    started = []

    def send(src, dst, to):
        i = used[0]
        used[0] += 1
        copy = pltpu.make_async_remote_copy(
            src_ref=src,
            dst_ref=dst,
            send_sem=s["send"].at[i],
            recv_sem=s["recv"].at[i],
            device_id=to,
            device_id_type=MESH,
        )
        copy.start()
        started.append(copy)
        return copy

    def local(src, dst):
        copy = pltpu.make_async_copy(src, dst, s["local"].at[used[1]])
        used[1] += 1
        copy.start()
        return copy

    def arrived(*copies):
        for copy in copies:
            copy.wait_recv()

    mine = pl.ds(pl.multiple_of(c * HALF, HALF), HALF)
    my_rows = pl.ds(pl.multiple_of(c * TOK, TOK), TOK)
    their_rows = pl.ds(pl.multiple_of(other * TOK, TOK), TOK)
    def head_row():
        return s["score"][...].astype(F32).reshape(1, 2 * HALF)

    def gain_row():
        return s["gain"][...].astype(F32).reshape(1, 2 * HALF)

    barrier = pltpu.get_barrier_semaphore()
    partners = (*to_p, *to_q, *to_xp, *to_xm, to_core, to_rep, to_both)
    for partner in partners:
        pl.semaphore_signal(barrier, inc=1, device_id=partner, device_id_type=MESH)

    local_in = [
        local(w_in.at[l, mine], s["wa", l].at[p, q, xl]) for l in range(LAYERS)
    ]
    local_out = [
        local(w_out.at[l, :, mine], s["own", l].at[pl.ds(0, R)]) for l in range(LAYERS)
    ]
    local_small = [
        local(src, s[name])
        for src, name in (
            (seg_ids, "seg"),
            (ranks, "ranks"),
            (score_head, "score"),
            (final_gain, "gain"),
        )
    ]

    hidden_sem = s["local"].at[31]

    def load_hidden(i, carry):
        yy, zz = i // 4, i % 4
        for xx in range(2):
            col = pl.multiple_of(yy * 2048 + xx * 1024 + zz * 256 + c * HALF, HALF)
            pltpu.make_async_copy(
                hidden.at[:, pl.ds(col, HALF)],
                s["h", 0].at[yy * other + zz * c, zz * other + yy * c, my_rows, pl.ds(xx * HALF, HALF)],
                hidden_sem,
            ).start()
        return carry

    lax.fori_loop(0, 16, load_hidden, 0)
    pl.semaphore_wait(barrier, len(partners))

    def gather_in(l):
        w, src = s["wa", l], w_in.at[l, mine]
        copies = [send(src, w.at[p, q, xl], to) for to in (to_q if l else (*to_q, *to_x))]
        yield
        local_in[l].wait()
        arrived(*copies)
        if l:
            copies = [
                send(w.at[p, low, xl], w.at[p, low, xl], to_xp[0]),
                send(w.at[p, high, xl], w.at[p, high, xl], to_xm[0]),
            ]
            yield
            arrived(*copies)
        a = send(w.at[p, low], w.at[p, low], to_p[0])
        b = send(w.at[p, high], w.at[p, high], to_p[2])
        copies = [
            send(w.at[p, high], w.at[p, high], to_p[0]),
            send(w.at[p, low], w.at[p, low], to_p[2]),
        ]
        yield
        arrived(a, b)
        copies += [
            send(w.at[pm, low], w.at[pm, low], to_p[0]),
            send(w.at[pp, high], w.at[pp, high], to_p[2]),
        ]
        yield
        arrived(*copies)
        yield

    def gather_out(l):
        w, own, rows = s["wb", l], s["own", l], unit_rows(l)
        local_out[l].wait()
        if rows > R:
            both = head_row() * gain_row()
            both = both[:, :HALF] * (1 - c).astype(F32) + both[:, HALF:] * c.astype(F32)
            hi = both.astype(BF16)
            lo = (both - hi.astype(F32)).astype(BF16)
            row = lax.broadcasted_iota(jnp.int32, (EXTRA, HALF), 0)
            own[pl.ds(R, EXTRA), :] = jnp.where(
                row == 0, hi.astype(F32), jnp.where(row == 1, lo.astype(F32), 0.0)
            ).astype(BF16)
        copies = [send(own, w.at[xl, p, q], to) for to in to_p]
        kept = local(own, w.at[xl, p, q])
        yield
        kept.wait()
        arrived(*copies)
        a = send(w.at[xl, low, q], w.at[xl, low, q], to_q[0])
        b = send(w.at[xl, high, q], w.at[xl, high, q], to_q[2])
        copies = [
            send(w.at[xl, high, q], w.at[xl, high, q], to_q[0]),
            send(w.at[xl, low, q], w.at[xl, low, q], to_q[2]),
        ]
        across = [
            send(w.at[xl, low, q], w.at[xl, low, q], to_xp[0]),
            send(w.at[xl, high, q], w.at[xl, high, q], to_xm[0]),
        ]
        yield
        arrived(a, b)
        copies += [
            send(w.at[xl, low, qm], w.at[xl, low, qm], to_q[0]),
            send(w.at[xl, high, qp], w.at[xl, high, qp], to_q[2]),
        ]
        across += [
            send(w.at[xl, low, qm], w.at[xl, low, qm], to_xp[0]),
            send(w.at[xl, high, qp], w.at[xl, high, qp], to_xm[0]),
        ]
        yield
        arrived(*copies)
        across += [
            send(w.at[xl, low, qp], w.at[xl, low, qp], to_xp[0]),
            send(w.at[xl, high, qm], w.at[xl, high, qm], to_xm[0]),
            send(w.at[xl, low, q2], w.at[xl, low, q2], to_xp[0]),
            send(w.at[xl, high, q2], w.at[xl, high, q2], to_xm[0]),
        ]
        yield
        arrived(*across)
        yield

    def total(*parts):
        value = parts[0].astype(F32)
        for part in parts[1:]:
            value = value + part.astype(F32)
        return value

    def finish(own, whole, far, l, store):
        copies = [send(own.at[xh], own.at[xh], to_rep)]
        if l == 0:
            copies += [send(own.at[xh], far.at[xh], to) for to in (to_core, to_both)]
        yield
        arrived(*copies)
        whole[c] = total(own[0], own[1])
        if l == 0:
            whole[other] = total(far[0], far[1])
        else:
            copy = send(whole.at[c], whole.at[c], to_core)
            yield
            arrived(copy)
        for half in range(2):
            store(l, half, whole[half])
        yield

    def scatter_out(l):
        g = s["gb", l]
        r1, r2, r3, r4, r5, r6, r7 = (s["gb%d" % i, l] for i in range(1, 8))
        across = []
        for j in (q2, qp, qm, q):
            if l == LAYERS - 1:
                top(j)
            partial(s["act_t", l], s["h", LAYERS], g, [(i, j) for i in range(4)])
            across += [
                send(g.at[1 - xl, low, j], r1.at[low, j], to_xp[0]),
                send(g.at[1 - xl, high, j], r1.at[high, j], to_xm[0]),
            ]
        yield
        arrived(*across[:2])
        for i in range(4):
            g[xl, i, q2] = total(g[xl, i, q2], r1[i, q2]).astype(BF16)
        a = send(g.at[xl, low, q2], r2.at[low], to_q[0])
        b = send(g.at[xl, high, q2], r2.at[high], to_q[2])
        yield
        arrived(*across[2:6])
        for i in range(2):
            g[xl, i + 2, qp] = total(g[xl, i + 2, qp], r1[i + 2, qp]).astype(BF16)
            g[xl, i, qm] = total(g[xl, i, qm], r1[i, qm]).astype(BF16)
        copies = [
            send(g.at[xl, high, qp], r3.at[0, high], to_q[0]),
            send(g.at[xl, low, qm], r3.at[1, low], to_q[2]),
        ]
        arrived(a, b)
        for i in range(2):
            g[xl, i, qp] = total(g[xl, i, qp], r1[i, qp], r2[i]).astype(BF16)
            g[xl, i + 2, qm] = total(g[xl, i + 2, qm], r1[i + 2, qm], r2[i + 2]).astype(BF16)
        copies += [
            send(g.at[xl, low, qp], r3.at[0, low], to_q[0]),
            send(g.at[xl, high, qm], r3.at[1, high], to_q[2]),
        ]
        yield
        arrived(*across[6:], *copies)
        for i in range(4):
            g[xl, i, q] = total(g[xl, i, q], r1[i, q], r3[0, i], r3[1, i]).astype(BF16)
        copies = [send(g.at[xl, (p + 1 + k) % 4, q], r4.at[k], to_p[k]) for k in range(3)]
        yield
        arrived(*copies)
        r5[xh] = total(g[xl, p, q], r4[0], r4[1], r4[2]).astype(BF16)
        yield from finish(r5, r6, r7, l, store_out)

    def scatter_in(l):
        g = s["ga", l]
        r1, r2, r3, r4, r5, r6 = (s["ga%d" % i, l] for i in range(1, 7))
        partial(s["dzr_t"], s["h", l], g, [(p2, j) for j in range(4)])
        a = send(g.at[:, p2, low], r1.at[:, low], to_p[0])
        b = send(g.at[:, p2, high], r1.at[:, high], to_p[2])
        partial(s["dzr_t"], s["h", l], g, [(pp, j) for j in (2, 3)] + [(pm, j) for j in (0, 1)])
        copies = [
            send(g.at[:, pp, high], r2.at[0, :, high], to_p[0]),
            send(g.at[:, pm, low], r2.at[1, :, low], to_p[2]),
        ]
        partial(s["dzr_t"], s["h", l], g, [(pp, j) for j in (0, 1)] + [(pm, j) for j in (2, 3)])
        partial(s["dzr_t"], s["h", l], g, [(p, j) for j in range(4)])
        yield
        arrived(a, b)
        for x in range(2):
            for j in range(2):
                g[x, pp, j] = total(g[x, pp, j], r1[x, j]).astype(BF16)
                g[x, pm, j + 2] = total(g[x, pm, j + 2], r1[x, j + 2]).astype(BF16)
        copies += [
            send(g.at[:, pp, low], r2.at[0, :, low], to_p[0]),
            send(g.at[:, pm, high], r2.at[1, :, high], to_p[2]),
        ]
        yield
        arrived(*copies)
        for x in range(2):
            for j in range(4):
                g[x, p, j] = total(g[x, p, j], r2[0, x, j], r2[1, x, j]).astype(BF16)
        copies = [send(g.at[xl, p, (q + 1 + k) % 4], r3.at[0, k + 1], to_q[k]) for k in range(3)]
        copies += [send(g.at[1 - xl, p, (q + k) % 4], r3.at[1, k], to_x[k]) for k in range(4)]
        yield
        arrived(*copies)
        r4[xh] = total(
            g[xl, p, q], *[r3[0, k] for k in range(1, 4)], *[r3[1, k] for k in range(4)]
        ).astype(BF16)
        yield from finish(r4, r5, r6, l, store_in)

    vecs, leaving = [], []

    def store_in(l, half, total):
        s["out_in"][l, pl.ds(half * HALF, HALF), :] = total.T
        if half == 1:
            leaving.append(local(s["out_in"].at[l], grad_in.at[l]))

    def store_out(l, half, total):
        lanes = pl.ds(half * HALF, HALF)
        s["out_out"][l, :, lanes] = total[:R]
        if half == 1:
            leaving.append(local(s["out_out"].at[l], grad_out.at[l]))
        if unit_rows(l) > R:
            vec = total[R : R + 8]
            row = lax.broadcasted_iota(jnp.int32, (8, HALF), 0)
            vec = jnp.sum(jnp.where(row == 0, vec, 0.0), axis=0, keepdims=True)
            vecs.append(vec)
            if half == 1:
                vec = jnp.concatenate(vecs, axis=1)
                s["out_head"][...] = (vec * gain_row()).reshape(2 * HALF)
                s["out_gain"][...] = (vec * head_row()).reshape(2 * HALF)
                leaving.append(local(s["out_head"], grad_head))
                leaving.append(local(s["out_gain"], grad_gain))

    def go(*jobs):
        for job in jobs:
            next(job, None)

    def lanes2(values):
        return jnp.concatenate([values, values], axis=1)

    def weights_out(l, i, j):
        w = s["wb", l]
        return jnp.concatenate([w[0, i, j, pl.ds(0, R)], w[1, i, j, pl.ds(0, R)]], axis=1)

    def squares(level):
        h, out = s["h", level], s["sq", level]
        out[...] = jnp.zeros_like(out)

        def step(i, carry):
            for r in range(0, ROWS, CHUNK):
                rows = pl.ds(r, CHUNK)
                total = out[rows, :]
                for j in range(4):
                    v = h[i, j, rows, :].astype(F32)
                    v = v * v
                    total = total + (v[:, :128] + v[:, 128:])
                out[rows, :] = total
            return carry

        lax.fori_loop(0, 4, step, 0)

    def down(l):
        h, w, out = s["h", l], s["wa", l], s["z", l]
        out[...] = jnp.zeros_like(out)

        def step(i, carry):
            lhs = jnp.concatenate([h[i, j] for j in range(4)], axis=1)
            out[...] += jnp.dot(lhs, w[i].reshape(4 * 2 * HALF, R), preferred_element_type=F32)
            return carry

        lax.fori_loop(0, 4, step, 0)

    def inverse(level):
        total = jnp.sum(s["sq", level][...] + s["sq_in", level][...], axis=1, keepdims=True)
        inv = lax.rsqrt(total * (1.0 / WIDTH) + EPS)
        s["rinv", level][...] = jnp.broadcast_to(inv, (ROWS, 128))

    def activate(l):
        v = (s["z", l][...] + s["z_in", l][...]) * s["rinv", l][...]
        s["z_in", l][...] = v
        active = v * jax.nn.sigmoid(v)
        s["act"][...] = active.astype(BF16)
        s["act_t", l][...] = active.T.astype(BF16)

    def up(l):
        h, out, sq = s["h", l], s["h", l + 1], s["sq", l + 1]
        last = l == LAYERS - 1
        sq[...] = jnp.zeros_like(sq)
        if last:
            s["q"][...] = jnp.zeros_like(s["q"])

        def step(i, carry):
            for j in range(4):
                w = weights_out(l, i, j)
                if last:
                    hg = s["hg"][i, j, 0:1, :]
                for r in range(0, ROWS, CHUNK):
                    rows = pl.ds(r, CHUNK)
                    v = jnp.dot(s["act"][rows, :], w, preferred_element_type=F32)
                    v = (h[i, j, rows, :].astype(F32) + v).astype(BF16)
                    out[i, j, rows, :] = v
                    v = v.astype(F32)
                    if last:
                        t = v * hg
                        s["q"][rows, :] += t[:, :128] + t[:, 128:]
                    v = v * v
                    sq[rows, :] += v[:, :128] + v[:, 128:]
            return carry

        lax.fori_loop(0, 4, step, 0)

    def gains():
        w = s["wb", LAYERS - 1]

        def step(i, carry):
            for j in range(4):
                for x in range(2):
                    rows = w[x, i, j, pl.ds(R, EXTRA)].astype(F32)
                    both = jnp.sum(rows, axis=0, keepdims=True)
                    s["hg"][i, j, :, pl.ds(x * HALF, HALF)] = jnp.broadcast_to(both, (8, HALF))
            return carry

        lax.fori_loop(0, 4, step, 0)

    def head():
        inv = s["rinv", LAYERS][...]
        dot_q = jnp.sum(s["q"][...] + s["q_in"][...], axis=1, keepdims=True)
        n_q = dot_q * inv
        seg_row = lax.broadcasted_iota(jnp.int32, (16, TOK), 0).astype(F32)
        onehots, rewards, counts = [], [], []
        for core in range(2):
            onehot = (s["packs"][core, 2:3, :] == seg_row).astype(F32)
            count = jnp.sum(onehot, axis=1, keepdims=True)
            total = jnp.dot(
                onehot,
                n_q[core * TOK : (core + 1) * TOK],
                precision=lax.Precision.HIGHEST,
                preferred_element_type=F32,
            )
            onehots.append(onehot)
            counts.append(count)
            rewards.append(total / count)
        place = lax.broadcasted_iota(jnp.int32, (8, 128), 0)
        lane = lax.broadcasted_iota(jnp.int32, (8, 128), 1)
        real = lane < 8
        for core in range(2):
            d_reward = []
            for k in range(2):
                order = s["packs"][core, 3 + k : 4 + k, 0:128]
                chosen = jnp.where(real & (order == place.astype(F32)), 1.0, 0.0)
                reward = rewards[core][8 * k : 8 * k + 8]
                placed = jnp.sum(chosen * reward, axis=0, keepdims=True)
                expo = jnp.exp(placed)
                suffix = jnp.sum(
                    jnp.where(real & (lane >= place), expo, 0.0), axis=1, keepdims=True
                )
                prefix = jnp.sum(
                    jnp.where(place <= lane, 1.0 / suffix, 0.0), axis=0, keepdims=True
                )
                d_placed = -1.0 + expo * prefix
                d_reward.append(
                    jnp.sum(jnp.where(chosen > 0.0, d_placed, 0.0), axis=1, keepdims=True)
                )
            scaled = jnp.concatenate(d_reward, axis=0) / counts[core]
            coef = lax.dot_general(
                onehots[core],
                jnp.broadcast_to(scaled, (16, 128)),
                (((0,), (0,)), ((), ())),
                precision=lax.Precision.HIGHEST,
                preferred_element_type=F32,
            )
            rows = pl.ds(core * TOK, TOK)
            inv_c = inv[core * TOK : (core + 1) * TOK]
            first = coef * inv_c
            s["coef"][rows, :] = first
            s["tok"][rows, :] = (
                first * inv_c * inv_c * dot_q[core * TOK : (core + 1) * TOK] * (1.0 / WIDTH)
            )
        vec = s["coef"][...].T[:8]
        hi = vec.astype(BF16)
        lo = (vec - hi.astype(F32)).astype(BF16)
        s["vec"][...] = jnp.concatenate([hi.astype(F32), lo.astype(F32)], axis=0).astype(BF16)

    def top(j):
        h, g = s["h", LAYERS], s["gb", LAYERS - 1]
        row = lax.broadcasted_iota(jnp.int32, (EXTRA, 256), 0)
        for i in range(4):
            vec = jnp.dot(s["vec"][...], h[i, j], preferred_element_type=F32)
            vec = jnp.where(row == 0, vec[0:1] + vec[8:9], 0.0).astype(BF16)
            g[0, i, j, pl.ds(R, EXTRA)] = vec[:, :HALF]
            g[1, i, j, pl.ds(R, EXTRA)] = vec[:, HALF:]
            hg = s["hg"][i, j, 0:1, :]
            for r in range(0, ROWS, CHUNK):
                rows = pl.ds(r, CHUNK)
                v = h[i, j, rows, :].astype(F32)
                v = lanes2(s["coef"][rows, :]) * hg - v * lanes2(s["tok"][rows, :])
                h[i, j, rows, :] = v.astype(BF16)

    def back_up(l):
        g, out = s["h", LAYERS], s["da", l]
        out[...] = jnp.zeros_like(out)

        def step(i, carry):
            lhs = jnp.concatenate([g[i, j] for j in range(4)], axis=1)
            rhs = jnp.concatenate([weights_out(l, i, j) for j in range(4)], axis=1)
            out[...] += lax.dot_general(lhs, rhs, NT, preferred_element_type=F32)
            return carry

        lax.fori_loop(0, 4, step, 0)

    def partial(lhs, wide, out, blocks):
        for i, j in blocks:
            v = jnp.dot(lhs[...], wide[i, j], preferred_element_type=F32).astype(BF16)
            out[0, i, j, pl.ds(0, R)] = v[:, :HALF]
            out[1, i, j, pl.ds(0, R)] = v[:, HALF:]

    def inner(l):
        v = s["z_in", l][...]
        inv = s["rinv", l][...]
        sigm = jax.nn.sigmoid(v)
        dz = (s["da", l][...] + s["da_in", l][...]) * sigm * (1.0 + v * (1.0 - sigm))
        mean = jnp.sum(dz * v, axis=1, keepdims=True) * (1.0 / WIDTH)
        s["tok"][...] = inv * inv * mean
        dz = dz * inv
        s["dzr"][...] = dz.astype(BF16)
        s["dzr_t"][...] = dz.T.astype(BF16)

    def back_down(l):
        g, h, w = s["h", LAYERS], s["h", l], s["wa", l]

        def step(i, carry):
            for j in range(4):
                rhs = w[i, j].reshape(2 * HALF, R)
                for r in range(0, ROWS, CHUNK):
                    rows = pl.ds(r, CHUNK)
                    du = lax.dot_general(s["dzr"][rows, :], rhs, NT, preferred_element_type=F32)
                    v = h[i, j, rows, :].astype(F32) * lanes2(s["tok"][rows, :])
                    g[i, j, rows, :] = (g[i, j, rows, :].astype(F32) + (du - v)).astype(BF16)
            return carry

        lax.fori_loop(0, 4, step, 0)

    in0, in1, in2 = (gather_in(l) for l in range(LAYERS))
    out0, out1, out2 = (gather_out(l) for l in range(LAYERS))
    core_send, core_recv = s["send"].at[N_SEMS - 1], s["recv"].at[N_SEMS - 1]
    def core_copy(src, dst):
        return pltpu.make_async_remote_copy(
            src_ref=src,
            dst_ref=dst,
            send_sem=core_send,
            recv_sem=core_recv,
            device_id=to_core,
            device_id_type=MESH,
        )
    go(in0)
    go(out0)
    def swap_hidden(i, carry):
        yy, zz = i // 4, i % 4
        for xx in range(2):
            col = pl.multiple_of(yy * 2048 + xx * 1024 + zz * 256 + other * HALF, HALF)
            core_copy(
                hidden.at[:, pl.ds(col, HALF)],
                s["h", 0].at[yy * c + zz * other, zz * c + yy * other, my_rows, pl.ds(xx * HALF, HALF)],
            ).start()
        return carry
    lax.fori_loop(0, 16, swap_hidden, 0)
    go(in1)
    go(out1)
    for copy in local_small:
        copy.wait()
    go(in2)
    go(out2)
    s["packs"][c, 2:3, :] = s["seg"][...].astype(F32)
    s["packs"][c, 3:5, 0:8] = s["ranks"][0].astype(F32)
    packs = send(s["packs"].at[c], s["packs"].at[c], to_core)
    go(in0)
    go(out0)
    go(in1)
    go(out1)
    go(in2)
    go(out2)
    go(in0)
    go(out0)
    go(in1)
    block = s["h", 0].at[:, :, my_rows]
    pltpu.make_async_copy(block, block, hidden_sem).wait()
    swapped = core_copy(block, s["h", 0].at[:, :, their_rows])
    swapped.wait_recv()
    swapped.wait_send()
    squares(0)
    sq = send(s["sq", 0], s["sq_in", 0], to_core)
    go(out1)
    go(in2)
    arrived(sq)
    inverse(0)
    go(out0)
    go(in0)
    down(0)
    zc = send(s["z", 0], s["z_in", 0], to_core)
    go(in1)
    go(out1)
    go(out2)
    arrived(zc)
    activate(0)
    go(out0)
    up(0)
    sq = send(s["sq", 1], s["sq_in", 1], to_core)
    go(in1)
    go(in2)
    go(out2)
    down(1)
    zc = send(s["z", 1], s["z_in", 1], to_core)
    arrived(sq)
    inverse(1)
    arrived(zc)
    activate(1)
    go(out1)
    up(1)
    sq = send(s["sq", 2], s["sq_in", 2], to_core)
    go(in2)
    down(2)
    zc = send(s["z", 2], s["z_in", 2], to_core)
    arrived(sq)
    inverse(2)
    arrived(zc)
    activate(2)
    go(out2)
    gains()
    up(2)
    sq = send(s["sq", 3], s["sq_in", 3], to_core)
    qc = send(s["q"], s["q_in"], to_core)
    arrived(packs, sq)
    inverse(3)
    arrived(qc)
    head()
    out2 = scatter_out(2)
    go(out2)
    back_up(2)
    dc = send(s["da", 2], s["da_in", 2], to_core)
    arrived(dc)
    inner(2)
    in2 = scatter_in(2)
    go(in2)
    back_down(2)
    go(out2)
    back_up(1)
    dc = send(s["da", 1], s["da_in", 1], to_core)
    out1 = scatter_out(1)
    go(out1)
    go(in2)
    go(out2)
    arrived(dc)
    inner(1)
    in1 = scatter_in(1)
    go(in1)
    go(out1)
    back_down(1)
    go(in2)
    go(out2)
    back_up(0)
    dc = send(s["da", 0], s["da_in", 0], to_core)
    out0 = scatter_out(0)
    go(out0)
    go(in1)
    go(out1)
    arrived(dc)
    inner(0)
    in0 = scatter_in(0)
    go(in0)
    go(out0)
    go(out2)
    go(in1)
    go(out1)
    go(in0)
    go(out0)
    go(in2)
    go(out2)
    go(in1)
    go(in2)
    go(out1)
    go(out2)
    go(in0)
    go(out0)
    go(in1)
    go(in2)
    go(out1)
    go(in0)
    go(out0)
    go(in1)
    go(out1)
    go(in0)
    go(out0)
    go(in0)
    go(out0)
    for copy in started:
        copy.wait_send()
    for copy in leaving:
        copy.wait()

def deliver(*refs):
    came, went = refs[-2], refs[-1]
    pieces = [(i, l) for l in range(LAYERS) for i in range(2)] + [(2, None), (3, None)]

    def part(ref, l):
        return ref if l is None else ref.at[l]

    reads = [
        pltpu.make_async_copy(part(refs[i], l), part(refs[i + 8], l), came.at[k])
        for k, (i, l) in enumerate(pieces)
    ]
    writes = [
        pltpu.make_async_copy(part(refs[i + 8], l), part(refs[i + 4], l), went.at[k])
        for k, (i, l) in enumerate(pieces)
    ]
    for copy in reads:
        copy.start()
    for read, write in zip(reads, writes):
        read.wait()
        write.start()
    for copy in writes:
        copy.wait()

def body(hidden, seg_ids, ranks, adapter_in, adapter_out, score_head, final_gain):
    hbm = pl.BlockSpec(memory_space=pl.ANY)
    shapes = (
        jax.ShapeDtypeStruct((LAYERS, 2 * HALF, R), F32),
        jax.ShapeDtypeStruct((LAYERS, R, 2 * HALF), F32),
        jax.ShapeDtypeStruct((2 * HALF,), F32),
        jax.ShapeDtypeStruct((2 * HALF,), F32),
    )
    grads = pl.pallas_call(
        kernel,
        out_shape=shapes,
        in_specs=[hbm] * 7,
        out_specs=(hbm,) * 4,
        scratch_shapes=list(scratch().values()),
        compiler_params=pltpu.CompilerParams(
            collective_id=0, has_side_effects=True, vmem_limit_bytes=60 * 1024 * 1024
        ),
        name="adapters",
    )(hidden, seg_ids, ranks, adapter_in, adapter_out, score_head, final_gain)
    return pl.pallas_call(
        deliver,
        out_shape=shapes,
        in_specs=[hbm] * 4,
        out_specs=(hbm,) * 4,
        scratch_shapes=[pltpu.VMEM(x.shape, x.dtype) for x in shapes]
        + [pltpu.SemaphoreType.DMA((8,)), pltpu.SemaphoreType.DMA((8,))],
        compiler_params=pltpu.CompilerParams(vmem_limit_bytes=60 * 1024 * 1024),
        name="deliver",
    )(*grads)

def solution(mesh):
    placed = (
        P(("rep", "shard"), None),
        P(("rep", "shard"), None),
        P(("rep", "shard"), None, None),
        P(None, "shard", None),
        P(None, None, "shard"),
        P("shard"),
        P("shard"),
    )
    return jax.shard_map(
        body,
        mesh=mesh,
        in_specs=placed,
        out_specs=(P(None, "shard", None), P(None, None, "shard"), P("shard"), P("shard")),
        check_vma=False,
    )
```
